32 devices in a mesh: gz: 4 (over y, x), xy: 8 (over z, core).
Axes of the slice: x: 2, y: 2, z: 4, core: 2. Of those that a mesh axis runs over, the one named last changes fastest.
Arguments:
- residual_in: float32 [144, 32, 8, 128], P(None, 'gz', 'xy'), may hold values from -75 to 75
- ritz_vector: float32 [144, 32, 8, 128], P(None, 'gz', 'xy'), may hold values from -14.4 to 14.4
- density: float32 [32, 8, 128], P('gz', 'xy'), may hold values from 0 to 1
- pml_flags: int32 [32, 8, 128], P('gz', 'xy'), may hold values 0 or 1
- design_mask: int32 [32, 8, 128], P('gz', 'xy'), may hold values 0 or 1
- k_base: float32 [144, 144], replicated, may hold values from -0.5 to 4.5
- k_rho: float32 [144, 144], replicated, may hold values from -0.5 to 0.5
- k_pml: float32 [144, 144], replicated, may hold values from -0.5 to 0.5
- k_face: float32 [6, 144, 144], replicated, may hold values from -0.5 to 0.5
- shift_re: float32 [], replicated, may hold values from 0.5 to 2
- shift_im: float32 [], replicated, may hold values from 0.2 to 1
Outputs:
- correction: float32 [144, 32, 8, 128], P(None, 'gz', 'xy')
- filtered: float32 [32, 8, 128], P('gz', 'xy')
The draws below stay inside these ranges and needn't reach their ends.
All inputs are finite; a program needn't handle non-finite values. No bound on the sum of `pml_flags` or of `design_mask` on one device may be relied on, other than what follows from the above.
Results may differ from the reference program's by a relative error of at most 0.0055.
Values sent between devices are 32-bit elements; how exact they have to be, the bound alone decides.
A program may use at most 64 MiB of HBM per device.

```python
import math
import jax
import jax.numpy as jnp
from jax import lax

B = 144
TX = 4
EY = 8
EX = 16
TY = 2
TILES = 8
NZ = 32
ELEMS = 32768


mean_diagonal = 3.0 / math.log(4.0)


def ritz_common(key):
    values = jax.random.normal(jax.random.fold_in(key, 101), (B, 1, 1, 1), jnp.float32)
    return 0.8 * jnp.clip(values, -3.0, 3.0)


def depth_profile():
    layers = jnp.arange(NZ, dtype=jnp.float32)
    return (1.0 + layers / (NZ - 1.0))[None, :, None, None]


def random_field(key, number):
    field_shape = (B, NZ, TILES, EY * EX)
    return jnp.clip(jax.random.normal(jax.random.fold_in(key, number), field_shape, jnp.float32), -4.0, 4.0)


def ritz_field(key):
    return (ritz_common(key) + random_field(key, 102)) * depth_profile()


def base_diagonal(key):
    return jnp.exp(jax.random.uniform(jax.random.fold_in(key, 201), (B,), jnp.float32, 0.0, math.log(4.0)))


def draw_k_base(key, part):
    diagonal_part = base_diagonal(key)
    coupling = jnp.clip(jax.random.normal(jax.random.fold_in(key, 202), (B, B), jnp.float32) / 12.0, -0.5, 0.5)
    return coupling + jnp.eye(B, dtype=jnp.float32) * diagonal_part[None, :]


def draw_ritz_vector(key, part):
    return ritz_field(key)


def draw_residual_in(key, part):
    ritz = ritz_field(key)
    half_rows = B // 2
    turned = jnp.concatenate([-ritz[half_rows:], ritz[:half_rows]], axis=0)
    amplitude = jax.random.uniform(jax.random.fold_in(key, 301), (), jnp.float32, 0.5, 1.5)
    rotation = jax.random.uniform(jax.random.fold_in(key, 302), (), jnp.float32, -math.pi, math.pi)
    tilted = 1.5 * ritz_common(key) * (base_diagonal(key) - mean_diagonal)[:, None, None, None]
    aligned = amplitude * (jnp.cos(rotation) * ritz + jnp.sin(rotation) * turned)
    return (random_field(key, 303) + tilted) * depth_profile() + aligned


def with_ends(entries, rng, low, high):
    longest = entries.shape.index(max(entries.shape))
    spots = []
    for shift in (0, 1):
        where = [jax.random.randint(jax.random.fold_in(rng, axis), (), 0, length) for axis, length in enumerate(entries.shape)]
        where[longest] = (where[longest] + shift) % entries.shape[longest]
        spots.append(tuple(where))
    return entries.at[spots[0]].set(low).at[spots[1]].set(high)


def steps_of(rng, extent, cuts, smallest, largest):
    def one(position, shards_of):
        heights = jax.random.uniform(jax.random.fold_in(jax.random.fold_in(rng, 6), position), (shards_of,), jnp.float32, smallest / len(cuts), largest / len(cuts))
        return jnp.repeat(jnp.exp(heights), extent[position] // shards_of).reshape((-1,) + (1,) * (len(extent) - position - 1))

    level = one(*cuts[0])
    for cut in cuts[1:]:
        level = level * one(*cut)
    return level


def noise(key, extent, spread, bound, kind=jnp.bfloat16):
    array = jax.random.normal(key, extent, jnp.float32) * spread
    return jnp.minimum(jnp.maximum(array, -bound), bound).astype(kind)


def setup_inputs(seed: int = 0) -> dict:
    arg_keys = jax.random.split(jax.random.key(seed), 12)
    return {
        "residual_in": draw_residual_in(jax.random.fold_in(arg_keys[11], 71), 0),
        "ritz_vector": draw_ritz_vector(jax.random.fold_in(arg_keys[11], 71), 0),
        "density": jnp.clip(1.0 * jax.random.uniform(arg_keys[2], (NZ, TILES, EY * EX), jnp.float32) ** steps_of(arg_keys[2], (NZ, TILES, EY * EX), ((0, 4), (1, 8)), -0.2, 0.2), 0.0, 1.0),
        "pml_flags": with_ends((jax.random.randint(arg_keys[3], (NZ, TILES, EY * EX), 0, 4) < 1).astype(jnp.int32), jax.random.fold_in(arg_keys[3], 1), 0, 1),
        "design_mask": with_ends((jax.random.randint(arg_keys[4], (NZ, TILES, EY * EX), 0, 2) < 1).astype(jnp.int32), jax.random.fold_in(arg_keys[4], 1), 0, 1),
        "k_base": draw_k_base(jax.random.fold_in(arg_keys[11], 71), 0),
        "k_rho": noise(arg_keys[6], (B, B), B ** -0.5, 0.5, jnp.float32),
        "k_pml": noise(arg_keys[7], (B, B), B ** -0.5, 0.5, jnp.float32),
        "k_face": noise(arg_keys[8], (6, B, B), B ** -0.5, 0.5, jnp.float32),
        "shift_re": jnp.clip(jax.random.uniform(arg_keys[9], (), jnp.float32, 0.5, 2.0), 0.5, 2.0),
        "shift_im": jnp.clip(jax.random.uniform(arg_keys[10], (), jnp.float32, 0.2, 1.0), 0.2, 1.0),
    }


filter_reach = 5

def to_grid(values):
    leading = values.shape[:-3]
    count = len(leading)
    shaped = values.reshape(leading + (NZ, TY, TX, EY, EX))
    shaped = jnp.moveaxis(shaped, count + 3, count + 2)
    return shaped.reshape(leading + (NZ, TY * EY, TX * EX))

def from_grid(values):
    leading = values.shape[:-3]
    count = len(leading)
    shaped = values.reshape(leading + (NZ, TY, EY, TX, EX))
    shaped = jnp.moveaxis(shaped, count + 2, count + 3)
    return shaped.reshape(leading + (NZ, TILES, EY * EX))

def inner_pair(ritz, field):
    half = ritz.shape[0] // 2
    real_part = jnp.sum(ritz[:half] * field[:half] + ritz[half:] * field[half:])
    imag_part = jnp.sum(ritz[:half] * field[half:] - ritz[half:] * field[:half])
    return (real_part, imag_part)

def project_out(field, ritz, coef_re, coef_im):
    half = ritz.shape[0] // 2
    ritz_re = ritz[:half]
    ritz_im = ritz[half:]
    removed = jnp.concatenate([coef_re * ritz_re - coef_im * ritz_im, coef_re * ritz_im + coef_im * ritz_re], axis=0)
    return field - removed

def plane_product(matrix, plane):
    return jnp.einsum('ij,jbc->ibc', matrix, plane, precision=lax.Precision.HIGHEST)

def apply_shifted(field, density, pml_weight, k_base, k_rho, k_pml, k_face, shift_re, shift_im):
    padded = jnp.pad(field, ((0, 0), (1, 1), (1, 1), (1, 1)))
    half = field.shape[0] // 2

    def one_plane(index):
        window = lax.dynamic_slice_in_dim(padded, index, 3, axis=1)
        center = window[:, 1, 1:-1, 1:-1]
        dens_plane = lax.dynamic_index_in_dim(density, index, 0, keepdims=False)
        pml_plane = lax.dynamic_index_in_dim(pml_weight, index, 0, keepdims=False)
        rho_term = plane_product(k_rho, center)
        result = plane_product(k_base, center) + dens_plane * rho_term + pml_plane * plane_product(k_pml, center)
        neighbours = [window[:, 2, 1:-1, 1:-1], window[:, 0, 1:-1, 1:-1], window[:, 1, 2:, 1:-1], window[:, 1, :-2, 1:-1], window[:, 1, 1:-1, 2:], window[:, 1, 1:-1, :-2]]
        for number in range(6):
            result = result + plane_product(k_face[number], neighbours[number])
        real_part = center[:half]
        imag_part = center[half:]
        result = result - jnp.concatenate([shift_re * real_part - shift_im * imag_part, shift_re * imag_part + shift_im * real_part], axis=0)
        return (result, rho_term)
    planes, rho_planes = lax.map(one_plane, jnp.arange(field.shape[1], dtype=jnp.int32))
    return (jnp.moveaxis(planes, 0, 1), jnp.moveaxis(rho_planes, 0, 1))

def smooth_axis(values, axis):
    length = values.shape[axis]
    widths = [(filter_reach, filter_reach) if number == axis else (0, 0) for number in range(3)]
    padded = jnp.pad(values, widths)
    result = jnp.zeros(values.shape, jnp.float32)
    for offset in range(-filter_reach, filter_reach + 1):
        weight = (6.0 - abs(offset)) / 12.0
        result = result + weight * lax.slice_in_dim(padded, filter_reach + offset, filter_reach + offset + length, axis=axis)
    return result

def reference(residual_in, ritz_vector, density, pml_flags, design_mask, k_base, k_rho, k_pml, k_face, shift_re, shift_im):
    residual = to_grid(residual_in)
    ritz = to_grid(ritz_vector)
    dens = to_grid(density)
    pml_weight = to_grid(pml_flags.astype(jnp.float32))
    mask = to_grid(design_mask.astype(jnp.float32))
    ritz_norm = jnp.sum(ritz * ritz)
    first_re, first_im = inner_pair(ritz, residual)
    first = project_out(residual, ritz, first_re / ritz_norm, first_im / ritz_norm)
    image_one, unused = apply_shifted(first, dens, pml_weight, k_base, k_rho, k_pml, k_face, shift_re, shift_im)
    one_re, one_im = inner_pair(ritz, image_one)
    projected = project_out(image_one, ritz, one_re / ritz_norm, one_im / ritz_norm)
    proj_sq = jnp.sum(projected * projected)
    second = projected * jnp.sqrt(B * ELEMS / proj_sq)
    image_two, rho_term = apply_shifted(second, dens, pml_weight, k_base, k_rho, k_pml, k_face, shift_re, shift_im)
    two_re, two_im = inner_pair(ritz, image_two)
    correction = project_out(image_two, ritz, two_re / ritz_norm, two_im / ritz_norm)
    sensitivity = lax.optimization_barrier(jnp.sum(correction * rho_term, axis=0)) / 36.0 * mask
    smoothed = smooth_axis(smooth_axis(smooth_axis(sensitivity, 0), 1), 2)
    return (from_grid(correction), from_grid(smoothed))
```

```python
import functools

import jax
import jax.numpy as jnp
from jax import lax
from jax.experimental import pallas as pl
from jax.experimental.pallas import tpu as pltpu
from jax.sharding import PartitionSpec as P

TX = 4
EY = 8
EX = 16
LANES = EY * EX
REACH = 5
MESH = pl.DeviceIdType.MESH
F32 = jnp.float32
BF16 = jnp.bfloat16


def split(x):
    hi = x.astype(BF16)
    return hi, (x - hi.astype(F32)).astype(BF16)


def fold(x):
    return jnp.sum(x.reshape(x.shape[0] // 8, 8, LANES), axis=0)


def pair_terms(u, f):
    half = u.shape[0] // 2
    ur, ui, fr, fi = u[:half], u[half:], f[:half], f[half:]
    return fold(ur * fr + ui * fi), fold(ur * fi - ui * fr)


def removed_part(u, re, im):
    half = u.shape[0] // 2
    ur, ui = u[:half], u[half:]
    return jnp.concatenate([re * ur - im * ui, re * ui + im * ur], axis=0)


def mm(a, b):
    return jnp.dot(a, b, preferred_element_type=F32)


def kernel(
    G, X, B, depth,
    res, rit, den, pml, msk, kb, kr, kp, kf, sre, sim,
    cor, fil,
    kface, kself, hsend, hrecv, V, H, I1, st, st2, p1, p2,
    sens, zrecv, zpad, lat, lrecv, wlat,
    s1s, s1r, s2s, s2r, hss, hrs, zss, zrs, lss, lrs,
):
    g = lax.axis_index("gz")
    t = lax.axis_index("xy")
    col = lax.rem(t, TX)
    row = t // TX
    TY = X // TX
    count = float(B * depth * LANES * G * X)

    def gz_peer(o):
        return {"gz": lax.rem(g + o + G, G)}

    def xy_peer(o):
        return {"xy": lax.rem(t + o + X, X)}

    barrier = pltpu.get_barrier_semaphore()
    for o in range(1, G):
        pl.semaphore_signal(barrier, inc=1, device_id=gz_peer(o), device_id_type=MESH)
    for o in range(1, X):
        pl.semaphore_signal(barrier, inc=1, device_id=xy_peer(o), device_id_type=MESH)

    def rlayer(ref, z):
        return ref[pl.ds(z, B, stride=depth), :]

    def remote(src, dst, ss, rs, dev):
        return pltpu.make_async_remote_copy(
            src_ref=src, dst_ref=dst, send_sem=ss, recv_sem=rs,
            device_id=dev, device_id_type=MESH,
        )

    def stage1(r):
        return [
            remote(st.at[r], p1.at[r, o - 1], s1s.at[r, o - 1], s1r.at[r, o - 1], gz_peer(o))
            for o in range(1, G)
        ]

    def stage2(r):
        return [
            remote(st2.at[r], p2.at[r, o - 1], s2s.at[r, o - 1], s2r.at[r, o - 1], xy_peer(o))
            for o in range(1, X)
        ]

    def sum_start(r, a, b, c):
        rows = [jnp.sum(v, axis=0, keepdims=True) for v in (a, b, c)]
        st[r] = jnp.concatenate(rows + [jnp.zeros((5, LANES), F32)], axis=0)
        for copy in stage1(r):
            copy.start()

    def sum_middle(r):
        for copy in stage1(r):
            copy.wait()
        total = st[r]
        for o in range(G - 1):
            total = total + p1[r, o]
        st2[r] = total
        for copy in stage2(r):
            copy.start()

    def sum_end(r):
        for copy in stage2(r):
            copy.wait()
        total = st2[r]
        for o in range(X - 1):
            total = total + p2[r, o]
        total = jnp.sum(total, axis=1, keepdims=True)
        return total[0:1], total[1:2], total[2:3]

    faces = [
        (gz_peer(-1), g > 0, g < G - 1),
        (gz_peer(1), g < G - 1, g > 0),
        (xy_peer(-TX), row > 0, row < TY - 1),
        (xy_peer(TX), row < TY - 1, row > 0),
        (xy_peer(-1), col > 0, col < TX - 1),
        (xy_peer(1), col < TX - 1, col > 0),
    ]

    def halo(s, k):
        src = hsend.at[s, k]
        if s == 2 and k < 2:
            src = I1.at[0 if k == 0 else depth - 1]
        return remote(src, hrecv.at[s, k], hss.at[s, k], hrs.at[s, k], faces[k][0])

    def halo_start(s, ks):
        for k in ks:
            @pl.when(faces[k][1])
            def _(k=k):
                halo(s, k).start()

    def halo_wait(s):
        for k in range(6):
            @pl.when(faces[k][1])
            def _(k=k):
                halo(s, k).wait_send()

            @pl.when(faces[k][2])
            def _(k=k):
                halo(s, k).wait_recv()

    lane = lax.broadcasted_iota(jnp.int32, (B, LANES), 1)
    lane_x = lane % EX
    lane_y = lane // EX

    def pack(s, load):
        def step(z, carry):
            a, b, c, d = carry
            f = load(z)
            in_y = lane_y == z
            in_x = lane_x == z
            a = jnp.where(in_y, pltpu.roll(f, EX * z, 1), a)
            b = jnp.where(in_y, pltpu.roll(f, lax.rem(EX * z + EX, LANES), 1), b)
            c = jnp.where(in_x, pltpu.roll(f, z, 1), c)
            d = jnp.where(in_x, pltpu.roll(f, lax.rem(z + LANES - EX + 1, LANES), 1), d)
            return a, b, c, d

        def loop(z, carry):
            hs = step(z, tuple(hsend[s, 2 + k] for k in range(4)))
            for k in range(4):
                hsend[s, 2 + k] = hs[k]
            return carry

        for k in range(4):
            hsend[s, 2 + k] = jnp.zeros((B, LANES), F32)
        lax.fori_loop(0, depth, loop, 0)

    half_rows = B * depth // 2
    chunk = half_rows // 8

    def first_sums(i, carry):
        a, b, c = carry
        lo = pl.ds(pl.multiple_of(i * chunk, 8), chunk)
        hi = pl.ds(pl.multiple_of(half_rows + i * chunk, 8), chunk)
        ur, ui, fr, fi = rit[lo, :], rit[hi, :], res[lo, :], res[hi, :]
        return (
            a + fold(ur * ur + ui * ui),
            b + fold(ur * fr + ui * fi),
            c + fold(ur * fi - ui * fr),
        )

    zero = jnp.zeros((8, LANES), F32)
    sums = lax.fori_loop(0, 8, first_sums, (zero, zero, zero))
    pl.semaphore_wait(barrier, G - 1 + X - 1)
    sum_start(0, *sums)

    for s, ref in ((0, res), (1, rit)):
        hsend[s, 0] = rlayer(ref, 0)
        hsend[s, 1] = rlayer(ref, depth - 1)
        halo_start(s, (0, 1))
        pack(s, functools.partial(rlayer, ref))
        halo_start(s, (2, 3, 4, 5))
    sum_middle(0)

    for k in range(6):
        @pl.when(jnp.logical_not(faces[k][2]))
        def _(k=k):
            for s in range(3):
                hrecv[s, k] = jnp.zeros((B, LANES), F32)

    fh, fl = split(jnp.concatenate([kf[n] for n in range(6)], axis=1))
    kface[0:B, :] = fh
    kface[B:2 * B, :] = fl
    ri = lax.broadcasted_iota(jnp.int32, (B, B), 0)
    ci = lax.broadcasted_iota(jnp.int32, (B, B), 1)
    half = B // 2
    shift = (
        jnp.where(ri == ci, sre[0, 0], 0.0)
        + jnp.where(ri == ci + half, sim[0, 0], 0.0)
        - jnp.where(ri + half == ci, sim[0, 0], 0.0)
    )
    for n, block in enumerate((kb[...] - shift, kr[...], kp[...])):
        bh, bl = split(block)
        kself[n * B:(n + 1) * B, :] = bh
        kself[(n + 3) * B:(n + 4) * B, :] = bl

    ci = lax.broadcasted_iota(jnp.int32, (LANES, LANES), 0)
    co = lax.broadcasted_iota(jnp.int32, (LANES, LANES), 1)
    for k in range(9):
        dy, dx = k // 3 - 1, k % 3 - 1
        oy = jnp.abs(ci // EX + EY * dy - co // EX)
        ox = jnp.abs(ci % EX + EX * dx - co % EX)
        w = jnp.maximum(REACH + 1 - oy, 0) * jnp.maximum(REACH + 1 - ox, 0)
        wlat[k * LANES:(k + 1) * LANES, :] = w.astype(F32).astype(BF16)

    def build(s, load, scale, re, im):
        def layer(z, carry):
            V[z + 1] = scale * (load(z) - removed_part(rlayer(rit, z), re, im))
            return carry

        lax.fori_loop(0, depth, layer, 0)
        halo_wait(s)
        for k in range(6):
            h = scale * (hrecv[s, k] - removed_part(hrecv[1, k], re, im))
            if k == 0:
                V[depth + 1] = h
            elif k == 1:
                V[0] = h
            else:
                H[k - 2] = h

    def image(j):
        lists = [[], [], [], [], [], [], []]
        for q in range(2):
            z = 2 * j + q
            c = V[z + 1]
            yp = jnp.where(lane_y == EY - 1, pltpu.roll(H[0], LANES - EX - EX * z, 1), pltpu.roll(c, LANES - EX, 1))
            ym = jnp.where(lane_y == 0, pltpu.roll(H[1], lax.rem(LANES - EX * z, LANES), 1), pltpu.roll(c, EX, 1))
            xp = jnp.where(lane_x == EX - 1, pltpu.roll(H[2], EX - 1 - z, 1), pltpu.roll(c, LANES - 1, 1))
            xm = jnp.where(lane_x == 0, pltpu.roll(H[3], lax.rem(LANES - z, LANES), 1), pltpu.roll(c, 1, 1))
            for entry, v in zip(lists, (c, V[z + 2], V[z], yp, ym, xp, xm)):
                entry.append(v)
        parts = [split(jnp.concatenate(e, axis=1)) for e in lists]
        fh = jnp.concatenate([p[0] for p in parts[1:]], axis=0)
        fl = jnp.concatenate([p[1] for p in parts[1:]], axis=0)
        both = mm(kface[...], fh)
        total = both[:B] + both[B:] + mm(kface[0:B, :], fl)
        ch, cl = parts[0]
        own = mm(kself[0:3 * B, :], ch) + mm(kself[3 * B:6 * B, :], ch) + mm(kself[0:3 * B, :], cl)
        d = jnp.concatenate([den[pl.ds(2 * j, 1), :], den[pl.ds(2 * j + 1, 1), :]], axis=1)
        p = jnp.concatenate([pml[pl.ds(2 * j, 1), :], pml[pl.ds(2 * j + 1, 1), :]], axis=1).astype(F32)
        rho = own[B:2 * B]
        return total + own[:B] + d * rho + p * own[2 * B:], rho

    norm, re, im = sum_end(0)
    inv = 1.0 / norm
    halo_wait(1)
    build(0, functools.partial(rlayer, res), 1.0, re * inv, im * inv)

    def apply_one(j, carry):
        a, b, c = carry
        out, unused = image(j)
        for q in range(2):
            z = 2 * j + q
            o = out[:, q * LANES:(q + 1) * LANES]
            I1[z] = o
            re_q, im_q = pair_terms(rlayer(rit, z), o)
            a, b, c = a + re_q, b + im_q, c + fold(o * o)
        return a, b, c

    sums = lax.fori_loop(0, depth // 2, apply_one, (zero, zero, zero))
    sum_start(1, *sums)
    halo_start(2, (0, 1))
    pack(2, lambda z: I1[z])
    halo_start(2, (2, 3, 4, 5))
    sum_middle(1)
    re, im, square = sum_end(1)
    factor = jnp.sqrt(count / (square - (re * re + im * im) * inv))
    build(2, lambda z: I1[z], factor, re * inv, im * inv)

    def apply_two(j, carry):
        a, b = carry
        out, rho = image(j)
        for q in range(2):
            z = 2 * j + q
            o = out[:, q * LANES:(q + 1) * LANES]
            r = rho[:, q * LANES:(q + 1) * LANES]
            I1[z] = o
            u = rlayer(rit, z)
            re_q, im_q = pair_terms(u, o)
            a, b = a + re_q, b + im_q
            w = msk[pl.ds(z, 1), :].astype(F32) * (1.0 / 36.0)
            br, bi = pair_terms(u, r)
            for n, v in enumerate((fold(o * r), br, bi)):
                sens[n, pl.ds(z, 1), :] = jnp.sum(v, axis=0, keepdims=True) * w
        return a, b

    a, b = lax.fori_loop(0, depth // 2, apply_two, (zero, zero))
    sum_start(2, a, b, zero)

    def zcopy(k):
        return remote(sens, zrecv.at[k], zss.at[k], zrs.at[k], faces[k][0])

    for k in range(2):
        @pl.when(faces[k][1])
        def _(k=k):
            zcopy(k).start()

        @pl.when(jnp.logical_not(faces[k][2]))
        def _(k=k):
            zrecv[k] = jnp.zeros((3, depth, LANES), F32)

    sum_middle(2)
    for k in range(2):
        @pl.when(faces[k][1])
        def _(k=k):
            zcopy(k).wait_send()

        @pl.when(faces[k][2])
        def _(k=k):
            zcopy(k).wait_recv()
    for n in range(3):
        zpad[n, 0:depth, :] = zrecv[1, n]
        zpad[n, depth:2 * depth, :] = sens[n]
        zpad[n, 2 * depth:3 * depth, :] = zrecv[0, n]
        total = jnp.zeros((depth, LANES), F32)
        for d in range(-REACH, REACH + 1):
            total = total + ((REACH + 1.0 - abs(d)) / 12.0) * zpad[n, depth + d:2 * depth + d, :]
        lat[n * depth:(n + 1) * depth, :] = total

    lateral = []
    for k in range(9):
        if k == 4:
            continue
        dy, dx = k // 3 - 1, k % 3 - 1
        gets = (row + dy >= 0) & (row + dy < TY) & (col + dx >= 0) & (col + dx < TX)
        gives = (row - dy >= 0) & (row - dy < TY) & (col - dx >= 0) & (col - dx < TX)
        copy = remote(lat, lrecv.at[k], lss.at[k], lrs.at[k], xy_peer(-dy * TX - dx))
        lateral.append((k, gets, gives, copy))
    for k, gets, gives, copy in lateral:
        @pl.when(gives)
        def _(copy=copy):
            copy.start()

        @pl.when(jnp.logical_not(gets))
        def _(k=k):
            lrecv[k] = jnp.zeros((3 * depth, LANES), F32)
    lrecv[4] = lat[...]

    re, im, unused = sum_end(2)
    re, im = re * inv, im * inv

    def finish(z, carry):
        cor[pl.ds(z, B, stride=depth), :] = I1[z] - removed_part(rlayer(rit, z), re, im)
        return carry

    lax.fori_loop(0, depth, finish, 0)
    for k, gets, gives, copy in lateral:
        @pl.when(gives)
        def _(copy=copy):
            copy.wait_send()

        @pl.when(gets)
        def _(copy=copy):
            copy.wait_recv()
    tiles = jnp.concatenate([lrecv[k] for k in range(9)], axis=1)
    th, tl = split(tiles)
    smooth = (mm(th, wlat[...]) + mm(tl, wlat[...])) * (1.0 / 144.0)
    fil[...] = smooth[:depth] - re * smooth[depth:2 * depth] - im * smooth[2 * depth:]


def local(G, X, residual_in, ritz_vector, density, pml_flags, design_mask, k_base, k_rho, k_pml, k_face, shift_re, shift_im):
    B, depth = residual_in.shape[:2]
    vmem = pl.BlockSpec(memory_space=pltpu.VMEM)
    smem = pl.BlockSpec(memory_space=pltpu.SMEM)
    dma = pltpu.SemaphoreType.DMA
    field = (B, LANES)
    correction, filtered = pl.pallas_call(
        functools.partial(kernel, G, X, B, depth),
        out_shape=(
            jax.ShapeDtypeStruct((B * depth, LANES), F32),
            jax.ShapeDtypeStruct((depth, LANES), F32),
        ),
        in_specs=[vmem] * 9 + [smem] * 2,
        out_specs=(vmem, vmem),
        scratch_shapes=[
            pltpu.VMEM((2 * B, 6 * B), BF16),
            pltpu.VMEM((6 * B, B), BF16),
            pltpu.VMEM((3, 6) + field, F32),
            pltpu.VMEM((3, 6) + field, F32),
            pltpu.VMEM((depth + 2,) + field, F32),
            pltpu.VMEM((4,) + field, F32),
            pltpu.VMEM((depth,) + field, F32),
            pltpu.VMEM((3, 8, LANES), F32),
            pltpu.VMEM((3, 8, LANES), F32),
            pltpu.VMEM((3, G - 1, 8, LANES), F32),
            pltpu.VMEM((3, X - 1, 8, LANES), F32),
            pltpu.VMEM((3, depth, LANES), F32),
            pltpu.VMEM((2, 3, depth, LANES), F32),
            pltpu.VMEM((3, 3 * depth, LANES), F32),
            pltpu.VMEM((3 * depth, LANES), F32),
            pltpu.VMEM((9, 3 * depth, LANES), F32),
            pltpu.VMEM((9 * LANES, LANES), BF16),
            dma((3, G - 1)),
            dma((3, G - 1)),
            dma((3, X - 1)),
            dma((3, X - 1)),
            dma((3, 6)),
            dma((3, 6)),
            dma((2,)),
            dma((2,)),
            dma((9,)),
            dma((9,)),
        ],
        compiler_params=pltpu.CompilerParams(
            collective_id=0, has_side_effects=True, vmem_limit_bytes=40 * 1024 * 1024
        ),
    )(
        residual_in.reshape(B * depth, LANES),
        ritz_vector.reshape(B * depth, LANES),
        density.reshape(depth, LANES),
        pml_flags.reshape(depth, LANES),
        design_mask.reshape(depth, LANES),
        k_base, k_rho, k_pml, k_face,
        shift_re.reshape(1, 1), shift_im.reshape(1, 1),
    )
    return correction.reshape(residual_in.shape), filtered.reshape(density.shape)


def solution(mesh):
    wide = P(None, "gz", "xy", None)
    flat = P("gz", "xy", None)
    return jax.shard_map(
        functools.partial(local, mesh.shape["gz"], mesh.shape["xy"]),
        mesh=mesh,
        in_specs=(wide, wide, flat, flat, flat, P(), P(), P(), P(), P(), P()),
        out_specs=(wide, flat),
        check_vma=False,
    )
```

```python
import functools

import jax
import jax.numpy as jnp
from jax import lax
from jax.experimental import pallas as pl
from jax.experimental.pallas import tpu as pltpu
from jax.sharding import PartitionSpec as P

TX = 4
EY = 8
EX = 16
LANES = EY * EX
REACH = 5
MESH = pl.DeviceIdType.MESH
F32 = jnp.float32
BF16 = jnp.bfloat16


def split(x):
    hi = x.astype(BF16)
    return hi, (x - hi.astype(F32)).astype(BF16)


def fold(x):
    return jnp.sum(x.reshape(x.shape[0] // 8, 8, LANES), axis=0)


def pair_terms(u, f):
    half = u.shape[0] // 2
    ur, ui, fr, fi = u[:half], u[half:], f[:half], f[half:]
    return fold(ur * fr + ui * fi), fold(ur * fi - ui * fr)


def removed_part(u, re, im):
    half = u.shape[0] // 2
    ur, ui = u[:half], u[half:]
    return jnp.concatenate([re * ur - im * ui, re * ui + im * ur], axis=0)


def mm(a, b):
    return jnp.dot(a, b, preferred_element_type=F32)


def kernel(
    G, X, B, depth,
    res_in, rit_in, den_in, pml_in, msk_in, kb_in, kr_in, kp_in, kf_in, sre, sim,
    cor, fil,
    res, rit, den, pml, msk, kb, kr, kp, kf,
    kface, kedge, kself, hsend, hrecv, edge, V, I1, RHO, st, st2, p1, p2,
    sens, zrecv, zpad, lat, lrecv, wlat,
    ins, s1s, s1r, s2s, s2r, hss, hrs, zss, zrs, lss, lrs,
):
    g = lax.axis_index("gz")
    t = lax.axis_index("xy")
    col = lax.rem(t, TX)
    row = t // TX
    TY = X // TX
    count = float(B * depth * LANES * G * X)

    loads = [
        pltpu.make_async_copy(src, dst, ins.at[n])
        for n, (src, dst) in enumerate((
            (rit_in, rit), (res_in, res), (kf_in, kf), (kb_in, kb), (kr_in, kr), (kp_in, kp),
            (den_in, den), (pml_in, pml), (msk_in, msk),
        ))
    ]
    for copy in loads:
        copy.start()

    def gz_peer(o):
        return {"gz": lax.rem(g + o + G, G)}

    def xy_peer(o):
        return {"xy": lax.rem(t + o + X, X)}

    barrier = pltpu.get_barrier_semaphore()
    for o in range(1, G):
        pl.semaphore_signal(barrier, inc=1, device_id=gz_peer(o), device_id_type=MESH)
    for o in range(1, X):
        pl.semaphore_signal(barrier, inc=1, device_id=xy_peer(o), device_id_type=MESH)

    def rlayer(ref, z):
        return ref[pl.ds(z, B, stride=depth), :]

    def remote(src, dst, ss, rs, dev):
        return pltpu.make_async_remote_copy(
            src_ref=src, dst_ref=dst, send_sem=ss, recv_sem=rs,
            device_id=dev, device_id_type=MESH,
        )

    def stage1(r):
        return [
            remote(st.at[r], p1.at[r, o - 1], s1s.at[r, o - 1], s1r.at[r, o - 1], gz_peer(o))
            for o in range(1, G)
        ]

    def stage2(r):
        return [
            remote(st2.at[r], p2.at[r, o - 1], s2s.at[r, o - 1], s2r.at[r, o - 1], xy_peer(o))
            for o in range(1, X)
        ]

    def sum_start(r, a, b, c):
        rows = [jnp.sum(v, axis=0, keepdims=True) for v in (a, b, c)]
        st[r] = jnp.concatenate(rows + [jnp.zeros((5, LANES), F32)], axis=0)
        for copy in stage1(r):
            copy.start()

    def sum_middle(r):
        for copy in stage1(r):
            copy.wait()
        total = st[r]
        for o in range(G - 1):
            total = total + p1[r, o]
        st2[r] = total
        for copy in stage2(r):
            copy.start()

    def sum_end(r):
        for copy in stage2(r):
            copy.wait()
        total = st2[r]
        for o in range(X - 1):
            total = total + p2[r, o]
        total = jnp.sum(total, axis=1, keepdims=True)
        return total[0:1], total[1:2], total[2:3]

    faces = [
        (gz_peer(-1), g > 0, g < G - 1),
        (gz_peer(1), g < G - 1, g > 0),
        (xy_peer(-TX), row > 0, row < TY - 1),
        (xy_peer(TX), row < TY - 1, row > 0),
        (xy_peer(-1), col > 0, col < TX - 1),
        (xy_peer(1), col < TX - 1, col > 0),
    ]

    def halo(s, k):
        src = (V.at[1], V.at[depth])[k] if k < 2 else hsend.at[s, k - 2]
        return remote(src, hrecv.at[s, k], hss.at[s, k], hrs.at[s, k], faces[k][0])

    def halo_start(s, ks):
        for k in ks:
            @pl.when(faces[k][1])
            def _(k=k):
                halo(s, k).start()

    def halo_wait(s):
        for k in range(6):
            @pl.when(faces[k][1])
            def _(k=k):
                halo(s, k).wait_send()

            @pl.when(faces[k][2])
            def _(k=k):
                halo(s, k).wait_recv()

    lane = lax.broadcasted_iota(jnp.int32, (B, LANES), 1)
    lane_x = lane % EX
    lane_y = lane // EX

    def pack(s, z, f):
        in_y = lane_y == z
        in_x = lane_x == z
        turned = (
            (in_y, pltpu.roll(f, EX * z, 1)),
            (in_y, pltpu.roll(f, lax.rem(EX * z + EX, LANES), 1)),
            (in_x, pltpu.roll(f, z, 1)),
            (in_x, pltpu.roll(f, lax.rem(z + LANES - EX + 1, LANES), 1)),
        )
        for k, (where, v) in enumerate(turned):
            hsend[s, k] = jnp.where(where, v, hsend[s, k])

    half_rows = B * depth // 2
    chunk = half_rows // 8

    def first_sums(i, carry):
        a, b, c = carry
        lo = pl.ds(pl.multiple_of(i * chunk, 8), chunk)
        hi = pl.ds(pl.multiple_of(half_rows + i * chunk, 8), chunk)
        ur, ui, fr, fi = rit[lo, :], rit[hi, :], res[lo, :], res[hi, :]
        return (
            a + fold(ur * ur + ui * ui),
            b + fold(ur * fr + ui * fi),
            c + fold(ur * fi - ui * fr),
        )

    zero = jnp.zeros((8, LANES), F32)
    loads[0].wait()
    loads[1].wait()
    sums = lax.fori_loop(0, 8, first_sums, (zero, zero, zero))
    pl.semaphore_wait(barrier, G - 1 + X - 1)
    sum_start(0, *sums)

    blank = jnp.zeros((B, LANES), F32)
    for s in range(2):
        for k in range(4):
            hsend[s, k] = blank
    V[0] = blank
    V[depth + 1] = blank
    for k in range(6):
        @pl.when(jnp.logical_not(faces[k][2]))
        def _(k=k):
            for s in range(2):
                hrecv[s, k] = blank

    for copy in loads[2:]:
        copy.wait()

    fh, fl = split(jnp.concatenate([kf[n] for n in range(6)], axis=1))
    kface[0:B, :] = fh
    kface[B:2 * B, :] = fl
    sum_middle(0)
    for n in range(6):
        bh, bl = split(kf[n])
        kedge[n, 0:B, :] = bh
        kedge[n, B:2 * B, :] = bl
    ri = lax.broadcasted_iota(jnp.int32, (B, B), 0)
    ci = lax.broadcasted_iota(jnp.int32, (B, B), 1)
    half = B // 2
    shift = (
        jnp.where(ri == ci, sre[0, 0], 0.0)
        + jnp.where(ri == ci + half, sim[0, 0], 0.0)
        - jnp.where(ri + half == ci, sim[0, 0], 0.0)
    )
    for n, block in enumerate((kb[...] - shift, kr[...], kp[...])):
        bh, bl = split(block)
        kself[n * B:(n + 1) * B, :] = bh
        kself[(n + 3) * B:(n + 4) * B, :] = bl

    ci = lax.broadcasted_iota(jnp.int32, (LANES, LANES), 0)
    co = lax.broadcasted_iota(jnp.int32, (LANES, LANES), 1)
    for k in range(9):
        dy, dx = k // 3 - 1, k % 3 - 1
        oy = jnp.abs(ci // EX + EY * dy - co // EX)
        ox = jnp.abs(ci % EX + EX * dx - co % EX)
        w = jnp.maximum(REACH + 1 - oy, 0) * jnp.maximum(REACH + 1 - ox, 0)
        wlat[k * LANES:(k + 1) * LANES, :] = w.astype(F32).astype(BF16)

    def build(s, load, scale, re, im):
        def layer(z, carry):
            v = scale * (load(z) - removed_part(rlayer(rit, z), re, im))
            V[z + 1] = v
            pack(s, z, v)
            return carry

        lax.fori_loop(0, depth, layer, 0)
        halo_start(s, range(6))

    def rims(s):
        halo_wait(s)
        for k in range(6):
            hh, hl = split(hrecv[s, k])
            both = mm(kedge[k], hh)
            edge[k] = both[:B] + both[B:] + mm(kedge[k, 0:B, :], hl)
        I1[depth - 1] += edge[0]
        I1[0] += edge[1]

    def with_rims(z):
        return (
            I1[z]
            + jnp.where(lane_y == EY - 1, pltpu.roll(edge[2], LANES - EX - EX * z, 1), 0.0)
            + jnp.where(lane_y == 0, pltpu.roll(edge[3], lax.rem(LANES - EX * z, LANES), 1), 0.0)
            + jnp.where(lane_x == EX - 1, pltpu.roll(edge[4], EX - 1 - z, 1), 0.0)
            + jnp.where(lane_x == 0, pltpu.roll(edge[5], lax.rem(LANES - z, LANES), 1), 0.0)
        )

    def image(j):
        lists = [[], [], [], [], [], [], []]
        for q in range(2):
            z = 2 * j + q
            c = V[z + 1]
            yp = jnp.where(lane_y == EY - 1, 0.0, pltpu.roll(c, LANES - EX, 1))
            ym = jnp.where(lane_y == 0, 0.0, pltpu.roll(c, EX, 1))
            xp = jnp.where(lane_x == EX - 1, 0.0, pltpu.roll(c, LANES - 1, 1))
            xm = jnp.where(lane_x == 0, 0.0, pltpu.roll(c, 1, 1))
            for entry, v in zip(lists, (c, V[z + 2], V[z], yp, ym, xp, xm)):
                entry.append(v)
        parts = [split(jnp.concatenate(e, axis=1)) for e in lists]
        fh = jnp.concatenate([p[0] for p in parts[1:]], axis=0)
        fl = jnp.concatenate([p[1] for p in parts[1:]], axis=0)
        both = mm(kface[...], fh)
        total = both[:B] + both[B:] + mm(kface[0:B, :], fl)
        ch, cl = parts[0]
        own = mm(kself[0:3 * B, :], ch) + mm(kself[3 * B:6 * B, :], ch) + mm(kself[0:3 * B, :], cl)
        d = jnp.concatenate([den[pl.ds(2 * j, 1), :], den[pl.ds(2 * j + 1, 1), :]], axis=1)
        p = jnp.concatenate([pml[pl.ds(2 * j, 1), :], pml[pl.ds(2 * j + 1, 1), :]], axis=1).astype(F32)
        rho = own[B:2 * B]
        out = total + own[:B] + d * rho + p * own[2 * B:]
        for q in range(2):
            I1[2 * j + q] = out[:, q * LANES:(q + 1) * LANES]
        return rho

    norm, re, im = sum_end(0)
    inv = 1.0 / norm
    build(0, functools.partial(rlayer, res), 1.0, re * inv, im * inv)

    def apply_one(j, carry):
        image(j)
        return carry

    def sums_one(z, carry):
        a, b, c = carry
        o = with_rims(z)
        I1[z] = o
        re_z, im_z = pair_terms(rlayer(rit, z), o)
        return a + re_z, b + im_z, c + fold(o * o)

    lax.fori_loop(0, depth // 2, apply_one, 0)
    rims(0)
    sums = lax.fori_loop(0, depth, sums_one, (zero, zero, zero))
    sum_start(1, *sums)
    sum_middle(1)
    re, im, square = sum_end(1)
    factor = jnp.sqrt(count / (square - (re * re + im * im) * inv))
    build(1, lambda z: I1[z], factor, re * inv, im * inv)

    def apply_two(j, carry):
        rho = image(j)
        for q in range(2):
            RHO[2 * j + q] = rho[:, q * LANES:(q + 1) * LANES]
        return carry

    def sums_two(z, carry):
        a, b = carry
        o = with_rims(z)
        I1[z] = o
        r = RHO[z]
        u = rlayer(rit, z)
        re_z, im_z = pair_terms(u, o)
        w = msk[pl.ds(z, 1), :].astype(F32) * (1.0 / 36.0)
        br, bi = pair_terms(u, r)
        for n, v in enumerate((fold(o * r), br, bi)):
            sens[n, pl.ds(z, 1), :] = jnp.sum(v, axis=0, keepdims=True) * w
        return a + re_z, b + im_z

    lax.fori_loop(0, depth // 2, apply_two, 0)
    rims(1)
    a, b = lax.fori_loop(0, depth, sums_two, (zero, zero))
    sum_start(2, a, b, zero)

    def zcopy(k):
        return remote(sens, zrecv.at[k], zss.at[k], zrs.at[k], faces[k][0])

    for k in range(2):
        @pl.when(faces[k][1])
        def _(k=k):
            zcopy(k).start()

        @pl.when(jnp.logical_not(faces[k][2]))
        def _(k=k):
            zrecv[k] = jnp.zeros((3, depth, LANES), F32)

    sum_middle(2)
    for k in range(2):
        @pl.when(faces[k][1])
        def _(k=k):
            zcopy(k).wait_send()

        @pl.when(faces[k][2])
        def _(k=k):
            zcopy(k).wait_recv()
    for n in range(3):
        zpad[n, 0:depth, :] = zrecv[1, n]
        zpad[n, depth:2 * depth, :] = sens[n]
        zpad[n, 2 * depth:3 * depth, :] = zrecv[0, n]
        total = jnp.zeros((depth, LANES), F32)
        for d in range(-REACH, REACH + 1):
            total = total + ((REACH + 1.0 - abs(d)) / 12.0) * zpad[n, depth + d:2 * depth + d, :]
        lat[n * depth:(n + 1) * depth, :] = total

    lateral = []
    for k in range(9):
        if k == 4:
            continue
        dy, dx = k // 3 - 1, k % 3 - 1
        gets = (row + dy >= 0) & (row + dy < TY) & (col + dx >= 0) & (col + dx < TX)
        gives = (row - dy >= 0) & (row - dy < TY) & (col - dx >= 0) & (col - dx < TX)
        copy = remote(lat, lrecv.at[k], lss.at[k], lrs.at[k], xy_peer(-dy * TX - dx))
        lateral.append((k, gets, gives, copy))
    for k, gets, gives, copy in lateral:
        @pl.when(gives)
        def _(copy=copy):
            copy.start()

        @pl.when(jnp.logical_not(gets))
        def _(k=k):
            lrecv[k] = jnp.zeros((3 * depth, LANES), F32)
    lrecv[4] = lat[...]

    re, im, unused = sum_end(2)
    re, im = re * inv, im * inv

    def finish(z, carry):
        cor[pl.ds(z, B, stride=depth), :] = I1[z] - removed_part(rlayer(rit, z), re, im)
        return carry

    lax.fori_loop(0, depth, finish, 0)
    for k, gets, gives, copy in lateral:
        @pl.when(gives)
        def _(copy=copy):
            copy.wait_send()

        @pl.when(gets)
        def _(copy=copy):
            copy.wait_recv()
    tiles = jnp.concatenate([lrecv[k] for k in range(9)], axis=1)
    th, tl = split(tiles)
    smooth = (mm(th, wlat[...]) + mm(tl, wlat[...])) * (1.0 / 144.0)
    fil[...] = smooth[:depth] - re * smooth[depth:2 * depth] - im * smooth[2 * depth:]


def local(G, X, residual_in, ritz_vector, density, pml_flags, design_mask, k_base, k_rho, k_pml, k_face, shift_re, shift_im):
    B, depth = residual_in.shape[:2]
    vmem = pl.BlockSpec(memory_space=pltpu.VMEM)
    smem = pl.BlockSpec(memory_space=pltpu.SMEM)
    dma = pltpu.SemaphoreType.DMA
    field = (B, LANES)
    correction, filtered = pl.pallas_call(
        functools.partial(kernel, G, X, B, depth),
        out_shape=(
            jax.ShapeDtypeStruct((B * depth, LANES), F32),
            jax.ShapeDtypeStruct((depth, LANES), F32),
        ),
        in_specs=[pl.BlockSpec(memory_space=pltpu.HBM)] * 9 + [smem] * 2,
        out_specs=(vmem, vmem),
        scratch_shapes=[
            pltpu.VMEM((B * depth, LANES), F32),
            pltpu.VMEM((B * depth, LANES), F32),
            pltpu.VMEM((depth, LANES), F32),
            pltpu.VMEM((depth, LANES), jnp.int32),
            pltpu.VMEM((depth, LANES), jnp.int32),
            pltpu.VMEM((B, B), F32),
            pltpu.VMEM((B, B), F32),
            pltpu.VMEM((B, B), F32),
            pltpu.VMEM((6, B, B), F32),
            pltpu.VMEM((2 * B, 6 * B), BF16),
            pltpu.VMEM((6, 2 * B, B), BF16),
            pltpu.VMEM((6 * B, B), BF16),
            pltpu.VMEM((2, 4) + field, F32),
            pltpu.VMEM((2, 6) + field, F32),
            pltpu.VMEM((6,) + field, F32),
            pltpu.VMEM((depth + 2,) + field, F32),
            pltpu.VMEM((depth,) + field, F32),
            pltpu.VMEM((depth,) + field, F32),
            pltpu.VMEM((3, 8, LANES), F32),
            pltpu.VMEM((3, 8, LANES), F32),
            pltpu.VMEM((3, G - 1, 8, LANES), F32),
            pltpu.VMEM((3, X - 1, 8, LANES), F32),
            pltpu.VMEM((3, depth, LANES), F32),
            pltpu.VMEM((2, 3, depth, LANES), F32),
            pltpu.VMEM((3, 3 * depth, LANES), F32),
            pltpu.VMEM((3 * depth, LANES), F32),
            pltpu.VMEM((9, 3 * depth, LANES), F32),
            pltpu.VMEM((9 * LANES, LANES), BF16),
            dma((9,)),
            dma((3, G - 1)),
            dma((3, G - 1)),
            dma((3, X - 1)),
            dma((3, X - 1)),
            dma((2, 6)),
            dma((2, 6)),
            dma((2,)),
            dma((2,)),
            dma((9,)),
            dma((9,)),
        ],
        compiler_params=pltpu.CompilerParams(
            collective_id=0, has_side_effects=True, vmem_limit_bytes=64 * 1024 * 1024
        ),
    )(
        residual_in.reshape(B * depth, LANES),
        ritz_vector.reshape(B * depth, LANES),
        density.reshape(depth, LANES),
        pml_flags.reshape(depth, LANES),
        design_mask.reshape(depth, LANES),
        k_base, k_rho, k_pml, k_face,
        shift_re.reshape(1, 1), shift_im.reshape(1, 1),
    )
    return correction.reshape(residual_in.shape), filtered.reshape(density.shape)


def solution(mesh):
    wide = P(None, "gz", "xy", None)
    flat = P("gz", "xy", None)
    return jax.shard_map(
        functools.partial(local, mesh.shape["gz"], mesh.shape["xy"]),
        mesh=mesh,
        in_specs=(wide, wide, flat, flat, flat, P(), P(), P(), P(), P(), P()),
        out_specs=(wide, flat),
        check_vma=False,
    )
```

```python
import functools

import jax
import jax.numpy as jnp
from jax import lax
from jax.experimental import pallas as pl
from jax.experimental.pallas import tpu as pltpu
from jax.sharding import PartitionSpec as P

TX = 4
EY = 8
EX = 16
LANES = EY * EX
REACH = 5
MESH = pl.DeviceIdType.MESH
F32 = jnp.float32
BF16 = jnp.bfloat16


def split(x):
    hi = x.astype(BF16)
    return hi, (x - hi.astype(F32)).astype(BF16)


def fold(x):
    return jnp.sum(x.reshape(x.shape[0] // 8, 8, LANES), axis=0)


def pair_terms(u, f):
    half = u.shape[0] // 2
    ur, ui, fr, fi = u[:half], u[half:], f[:half], f[half:]
    return fold(ur * fr + ui * fi), fold(ur * fi - ui * fr)


def removed_part(u, re, im):
    half = u.shape[0] // 2
    ur, ui = u[:half], u[half:]
    return jnp.concatenate([re * ur - im * ui, re * ui + im * ur], axis=0)


def mm(a, b):
    return jnp.dot(a, b, preferred_element_type=F32)


def kernel(
    G, X, B, depth,
    res_in, rit_in, den_in, pml_in, msk_in, kb_in, kr_in, kp_in, kf_in, sre, sim,
    cor, fil,
    res, rit, den, pml, msk, kb, kr, kp, kf, R, U,
    kface, kself, hsend, hrecv, V, H, I1, st, st2, p1, p2,
    sens, zrecv, zpad, lat, lrecv, wlat,
    ins, s1s, s1r, s2s, s2r, hss, hrs, zss, zrs, lss, lrs,
):
    g = lax.axis_index("gz")
    t = lax.axis_index("xy")
    col = lax.rem(t, TX)
    row = t // TX
    TY = X // TX
    count = float(B * depth * LANES * G * X)

    loads = [
        pltpu.make_async_copy(src, dst, ins.at[n])
        for n, (src, dst) in enumerate((
            (rit_in, rit), (res_in, res), (kf_in, kf), (kb_in, kb), (kr_in, kr), (kp_in, kp),
            (den_in, den), (pml_in, pml), (msk_in, msk),
        ))
    ]
    for copy in loads:
        copy.start()

    def gz_peer(o):
        return {"gz": lax.rem(g + o + G, G)}

    def xy_peer(o):
        return {"xy": lax.rem(t + o + X, X)}

    barrier = pltpu.get_barrier_semaphore()
    for o in range(1, G):
        pl.semaphore_signal(barrier, inc=1, device_id=gz_peer(o), device_id_type=MESH)
    for o in range(1, X):
        pl.semaphore_signal(barrier, inc=1, device_id=xy_peer(o), device_id_type=MESH)

    def rlayer(ref, z):
        return ref[pl.ds(z, B, stride=depth), :]

    def remote(src, dst, ss, rs, dev):
        return pltpu.make_async_remote_copy(
            src_ref=src, dst_ref=dst, send_sem=ss, recv_sem=rs,
            device_id=dev, device_id_type=MESH,
        )

    def stage1(r):
        return [
            remote(st.at[r], p1.at[r, o - 1], s1s.at[r, o - 1], s1r.at[r, o - 1], gz_peer(o))
            for o in range(1, G)
        ]

    def stage2(r):
        return [
            remote(st2.at[r], p2.at[r, o - 1], s2s.at[r, o - 1], s2r.at[r, o - 1], xy_peer(o))
            for o in range(1, X)
        ]

    def sum_start(r, a, b, c):
        rows = [jnp.sum(v, axis=0, keepdims=True) for v in (a, b, c)]
        st[r] = jnp.concatenate(rows + [jnp.zeros((5, LANES), F32)], axis=0)
        for copy in stage1(r):
            copy.start()

    def sum_middle(r):
        for copy in stage1(r):
            copy.wait()
        total = st[r]
        for o in range(G - 1):
            total = total + p1[r, o]
        st2[r] = total
        for copy in stage2(r):
            copy.start()

    def sum_end(r):
        for copy in stage2(r):
            copy.wait()
        total = st2[r]
        for o in range(X - 1):
            total = total + p2[r, o]
        total = jnp.sum(total, axis=1, keepdims=True)
        return total[0:1], total[1:2], total[2:3]

    faces = [
        (gz_peer(-1), g > 0, g < G - 1),
        (gz_peer(1), g < G - 1, g > 0),
        (xy_peer(-TX), row > 0, row < TY - 1),
        (xy_peer(TX), row < TY - 1, row > 0),
        (xy_peer(-1), col > 0, col < TX - 1),
        (xy_peer(1), col < TX - 1, col > 0),
    ]

    def halo(s, k):
        src = (R, U, I1)[s].at[(0, depth - 1)[k]] if k < 2 else hsend.at[s, k - 2]
        return remote(src, hrecv.at[s, k], hss.at[s, k], hrs.at[s, k], faces[k][0])

    def halo_start(s, ks):
        for k in ks:
            @pl.when(faces[k][1])
            def _(k=k):
                halo(s, k).start()

    def halo_wait(s):
        for k in range(6):
            @pl.when(faces[k][1])
            def _(k=k):
                halo(s, k).wait_send()

            @pl.when(faces[k][2])
            def _(k=k):
                halo(s, k).wait_recv()

    lane = lax.broadcasted_iota(jnp.int32, (1, LANES), 1)
    lane_x = lane % EX
    lane_y = lane // EX

    def pack(s, load):
        def step(z, carry):
            a, b, c, d = carry
            f = load(z)
            in_y = lane_y == z
            in_x = lane_x == z
            a = jnp.where(in_y, pltpu.roll(f, EX * z, 1), a)
            b = jnp.where(in_y, pltpu.roll(f, lax.rem(EX * z + EX, LANES), 1), b)
            c = jnp.where(in_x, pltpu.roll(f, z, 1), c)
            d = jnp.where(in_x, pltpu.roll(f, lax.rem(z + LANES - EX + 1, LANES), 1), d)
            return a, b, c, d

        def loop(z, carry):
            hs = step(z, tuple(hsend[s, k] for k in range(4)))
            for k in range(4):
                hsend[s, k] = hs[k]
            return carry

        for k in range(4):
            hsend[s, k] = jnp.zeros((B, LANES), F32)
        lax.fori_loop(0, depth, loop, 0)

    half_rows = B * depth // 2
    chunk = half_rows // 8

    def first_sums(i, carry):
        a, b, c = carry
        lo = pl.ds(pl.multiple_of(i * chunk, 8), chunk)
        hi = pl.ds(pl.multiple_of(half_rows + i * chunk, 8), chunk)
        ur, ui, fr, fi = rit[lo, :], rit[hi, :], res[lo, :], res[hi, :]
        return (
            a + fold(ur * ur + ui * ui),
            b + fold(ur * fr + ui * fi),
            c + fold(ur * fi - ui * fr),
        )

    zero = jnp.zeros((8, LANES), F32)
    loads[0].wait()
    loads[1].wait()
    sums = lax.fori_loop(0, 8, first_sums, (zero, zero, zero))
    pl.semaphore_wait(barrier, G - 1 + X - 1)
    sum_start(0, *sums)

    for s, ref, layers in ((0, res, R), (1, rit, U)):
        for k, z in ((0, 0), (1, depth - 1)):
            layers[z] = rlayer(ref, z)
        halo_start(s, (0, 1))

        def turned(z, ref=ref, layers=layers):
            f = rlayer(ref, z)

            @pl.when((z > 0) & (z < depth - 1))
            def _():
                layers[z] = f

            return f

        pack(s, turned)
        halo_start(s, (2, 3, 4, 5))
        if s == 0:
            sum_middle(0)

    for k in range(6):
        @pl.when(jnp.logical_not(faces[k][2]))
        def _(k=k):
            for s in range(3):
                hrecv[s, k] = jnp.zeros((B, LANES), F32)

    for copy in loads[2:]:
        copy.wait()
    fh, fl = split(jnp.concatenate([kf[n] for n in range(6)], axis=1))
    kface[0:B, :] = fh
    kface[B:2 * B, :] = fl
    ri = lax.broadcasted_iota(jnp.int32, (B, B), 0)
    ci = lax.broadcasted_iota(jnp.int32, (B, B), 1)
    half = B // 2
    shift = (
        jnp.where(ri == ci, sre[0, 0], 0.0)
        + jnp.where(ri == ci + half, sim[0, 0], 0.0)
        - jnp.where(ri + half == ci, sim[0, 0], 0.0)
    )
    for n, block in enumerate((kb[...] - shift, kr[...], kp[...])):
        bh, bl = (v.astype(F32) for v in split(block))
        kself[n * B:(n + 1) * B, :] = jnp.concatenate([bh, bh, bl], axis=1).astype(BF16)

    ci = lax.broadcasted_iota(jnp.int32, (LANES, LANES), 0)
    co = lax.broadcasted_iota(jnp.int32, (LANES, LANES), 1)
    for k in range(9):
        dy, dx = k // 3 - 1, k % 3 - 1
        oy = jnp.abs(ci // EX + EY * dy - co // EX)
        ox = jnp.abs(ci % EX + EX * dx - co % EX)
        w = jnp.maximum(REACH + 1 - oy, 0) * jnp.maximum(REACH + 1 - ox, 0)
        wlat[k * LANES:(k + 1) * LANES, :] = w.astype(F32).astype(BF16)

    def build(s, load, scale, re, im):
        def layer(z, carry):
            V[z + 1] = scale * (load(z) - removed_part(U[z], re, im))
            return carry

        lax.fori_loop(0, depth, layer, 0)
        halo_wait(s)
        for k in range(6):
            h = scale * (hrecv[s, k] - removed_part(hrecv[1, k], re, im))
            if k == 0:
                V[depth + 1] = h
            elif k == 1:
                V[0] = h
            else:
                H[k - 2] = h

    def image(j):
        lists = [[], [], [], [], [], [], []]
        for q in range(2):
            z = 2 * j + q
            c = V[z + 1]
            yp = jnp.where(lane_y == EY - 1, pltpu.roll(H[0], LANES - EX - EX * z, 1), pltpu.roll(c, LANES - EX, 1))
            ym = jnp.where(lane_y == 0, pltpu.roll(H[1], lax.rem(LANES - EX * z, LANES), 1), pltpu.roll(c, EX, 1))
            xp = jnp.where(lane_x == EX - 1, pltpu.roll(H[2], EX - 1 - z, 1), pltpu.roll(c, LANES - 1, 1))
            xm = jnp.where(lane_x == 0, pltpu.roll(H[3], lax.rem(LANES - z, LANES), 1), pltpu.roll(c, 1, 1))
            for entry, v in zip(lists, (c, V[z + 2], V[z], yp, ym, xp, xm)):
                entry.append(v)
        parts = [split(jnp.concatenate(e, axis=1)) for e in lists]
        fh = jnp.concatenate([p[0] for p in parts[1:]], axis=0)
        fl = jnp.concatenate([p[1] for p in parts[1:]], axis=0)
        both = mm(kface[...], fh)
        total = both[:B] + both[B:] + mm(kface[0:B, :], fl)
        ch, cl = parts[0]
        own = mm(kself[...], jnp.concatenate([ch, cl, ch], axis=0))
        d = jnp.concatenate([den[pl.ds(2 * j, 1), :], den[pl.ds(2 * j + 1, 1), :]], axis=1)
        p = jnp.concatenate([pml[pl.ds(2 * j, 1), :], pml[pl.ds(2 * j + 1, 1), :]], axis=1).astype(F32)
        rho = own[B:2 * B]
        return total + own[:B] + d * rho + p * own[2 * B:], rho

    norm, re, im = sum_end(0)
    inv = 1.0 / norm
    halo_wait(1)
    build(0, lambda z: R[z], 1.0, re * inv, im * inv)

    def apply_one(j, carry):
        a, b, c = carry
        out, unused = image(j)
        for q in range(2):
            z = 2 * j + q
            o = out[:, q * LANES:(q + 1) * LANES]
            I1[z] = o
            re_q, im_q = pair_terms(U[z], o)
            a, b, c = a + re_q, b + im_q, c + fold(o * o)
        return a, b, c

    sums = lax.fori_loop(0, depth // 2, apply_one, (zero, zero, zero))
    sum_start(1, *sums)
    halo_start(2, (0, 1))
    pack(2, lambda z: I1[z])
    halo_start(2, (2, 3, 4, 5))
    sum_middle(1)
    re, im, square = sum_end(1)
    factor = jnp.sqrt(count / (square - (re * re + im * im) * inv))
    build(2, lambda z: I1[z], factor, re * inv, im * inv)

    def apply_two(j, carry):
        a, b = carry
        out, rho = image(j)
        for q in range(2):
            z = 2 * j + q
            o = out[:, q * LANES:(q + 1) * LANES]
            r = rho[:, q * LANES:(q + 1) * LANES]
            I1[z] = o
            u = U[z]
            re_q, im_q = pair_terms(u, o)
            a, b = a + re_q, b + im_q
            w = msk[pl.ds(z, 1), :].astype(F32) * (1.0 / 36.0)
            br, bi = pair_terms(u, r)
            for n, v in enumerate((fold(o * r), br, bi)):
                sens[n, pl.ds(z, 1), :] = jnp.sum(v, axis=0, keepdims=True) * w
        return a, b

    a, b = lax.fori_loop(0, depth // 2, apply_two, (zero, zero))
    sum_start(2, a, b, zero)

    def zcopy(k):
        return remote(sens, zrecv.at[k], zss.at[k], zrs.at[k], faces[k][0])

    for k in range(2):
        @pl.when(faces[k][1])
        def _(k=k):
            zcopy(k).start()

        @pl.when(jnp.logical_not(faces[k][2]))
        def _(k=k):
            zrecv[k] = jnp.zeros((3, depth, LANES), F32)

    sum_middle(2)
    for k in range(2):
        @pl.when(faces[k][1])
        def _(k=k):
            zcopy(k).wait_send()

        @pl.when(faces[k][2])
        def _(k=k):
            zcopy(k).wait_recv()
    for n in range(3):
        zpad[n, 0:depth, :] = zrecv[1, n]
        zpad[n, depth:2 * depth, :] = sens[n]
        zpad[n, 2 * depth:3 * depth, :] = zrecv[0, n]
        total = jnp.zeros((depth, LANES), F32)
        for d in range(-REACH, REACH + 1):
            total = total + ((REACH + 1.0 - abs(d)) / 12.0) * zpad[n, depth + d:2 * depth + d, :]
        lat[n * depth:(n + 1) * depth, :] = total

    lateral = []
    for k in range(9):
        if k == 4:
            continue
        dy, dx = k // 3 - 1, k % 3 - 1
        gets = (row + dy >= 0) & (row + dy < TY) & (col + dx >= 0) & (col + dx < TX)
        gives = (row - dy >= 0) & (row - dy < TY) & (col - dx >= 0) & (col - dx < TX)
        copy = remote(lat, lrecv.at[k], lss.at[k], lrs.at[k], xy_peer(-dy * TX - dx))
        lateral.append((k, gets, gives, copy))
    for k, gets, gives, copy in lateral:
        @pl.when(gives)
        def _(copy=copy):
            copy.start()

        @pl.when(jnp.logical_not(gets))
        def _(k=k):
            lrecv[k] = jnp.zeros((3 * depth, LANES), F32)
    lrecv[4] = lat[...]

    re, im, unused = sum_end(2)
    re, im = re * inv, im * inv

    def finish(z, carry):
        cor[pl.ds(z, B, stride=depth), :] = I1[z] - removed_part(U[z], re, im)
        return carry

    lax.fori_loop(0, depth, finish, 0)
    for k, gets, gives, copy in lateral:
        @pl.when(gives)
        def _(copy=copy):
            copy.wait_send()

        @pl.when(gets)
        def _(copy=copy):
            copy.wait_recv()
    tiles = jnp.concatenate([lrecv[k] for k in range(9)], axis=1)
    th, tl = split(tiles)
    smooth = (mm(th, wlat[...]) + mm(tl, wlat[...])) * (1.0 / 144.0)
    fil[...] = smooth[:depth] - re * smooth[depth:2 * depth] - im * smooth[2 * depth:]


def local(G, X, residual_in, ritz_vector, density, pml_flags, design_mask, k_base, k_rho, k_pml, k_face, shift_re, shift_im):
    B, depth = residual_in.shape[:2]
    vmem = pl.BlockSpec(memory_space=pltpu.VMEM)
    smem = pl.BlockSpec(memory_space=pltpu.SMEM)
    dma = pltpu.SemaphoreType.DMA
    field = (B, LANES)
    correction, filtered = pl.pallas_call(
        functools.partial(kernel, G, X, B, depth),
        out_shape=(
            pltpu.VMEM((B * depth, LANES), F32),
            pltpu.VMEM((depth, LANES), F32),
        ),
        in_specs=[pl.BlockSpec(memory_space=pltpu.HBM)] * 9 + [smem] * 2,
        out_specs=(vmem, vmem),
        scratch_shapes=[
            pltpu.VMEM((B * depth, LANES), F32),
            pltpu.VMEM((B * depth, LANES), F32),
            pltpu.VMEM((depth, LANES), F32),
            pltpu.VMEM((depth, LANES), jnp.int32),
            pltpu.VMEM((depth, LANES), jnp.int32),
            pltpu.VMEM((B, B), F32),
            pltpu.VMEM((B, B), F32),
            pltpu.VMEM((B, B), F32),
            pltpu.VMEM((6, B, B), F32),
            pltpu.VMEM((depth,) + field, F32),
            pltpu.VMEM((depth,) + field, F32),
            pltpu.VMEM((2 * B, 6 * B), BF16),
            pltpu.VMEM((3 * B, 3 * B), BF16),
            pltpu.VMEM((3, 4) + field, F32),
            pltpu.VMEM((3, 6) + field, F32),
            pltpu.VMEM((depth + 2,) + field, F32),
            pltpu.VMEM((4,) + field, F32),
            pltpu.VMEM((depth,) + field, F32),
            pltpu.VMEM((3, 8, LANES), F32),
            pltpu.VMEM((3, 8, LANES), F32),
            pltpu.VMEM((3, G - 1, 8, LANES), F32),
            pltpu.VMEM((3, X - 1, 8, LANES), F32),
            pltpu.VMEM((3, depth, LANES), F32),
            pltpu.VMEM((2, 3, depth, LANES), F32),
            pltpu.VMEM((3, 3 * depth, LANES), F32),
            pltpu.VMEM((3 * depth, LANES), F32),
            pltpu.VMEM((9, 3 * depth, LANES), F32),
            pltpu.VMEM((9 * LANES, LANES), BF16),
            dma((9,)),
            dma((3, G - 1)),
            dma((3, G - 1)),
            dma((3, X - 1)),
            dma((3, X - 1)),
            dma((3, 6)),
            dma((3, 6)),
            dma((2,)),
            dma((2,)),
            dma((9,)),
            dma((9,)),
        ],
        compiler_params=pltpu.CompilerParams(
            collective_id=0, has_side_effects=True, vmem_limit_bytes=40 * 1024 * 1024
        ),
    )(
        *(
            pltpu.with_memory_space_constraint(x, pltpu.HBM)
            for x in (
                residual_in.reshape(B * depth, LANES),
                ritz_vector.reshape(B * depth, LANES),
                density.reshape(depth, LANES),
                pml_flags.reshape(depth, LANES),
                design_mask.reshape(depth, LANES),
                k_base, k_rho, k_pml, k_face,
            )
        ),
        shift_re.reshape(1, 1), shift_im.reshape(1, 1),
    )
    return correction.reshape(residual_in.shape), filtered.reshape(density.shape)


def solution(mesh):
    wide = P(None, "gz", "xy", None)
    flat = P("gz", "xy", None)
    return jax.shard_map(
        functools.partial(local, mesh.shape["gz"], mesh.shape["xy"]),
        mesh=mesh,
        in_specs=(wide, wide, flat, flat, flat, P(), P(), P(), P(), P(), P()),
        out_specs=(wide, flat),
        check_vma=False,
    )
```

```python
import functools

import jax
import jax.numpy as jnp
from jax import lax
from jax.experimental import pallas as pl
from jax.experimental.pallas import tpu as pltpu
from jax.sharding import PartitionSpec as P

TX = 4
EY = 8
EX = 16
LANES = EY * EX
REACH = 5
MESH = pl.DeviceIdType.MESH
F32 = jnp.float32
BF16 = jnp.bfloat16


def split(x):
    hi = x.astype(BF16)
    return hi, (x - hi.astype(F32)).astype(BF16)


def fold(x):
    return jnp.sum(x.reshape(x.shape[0] // 8, 8, LANES), axis=0)


def pair_terms(u, f):
    half = u.shape[0] // 2
    ur, ui, fr, fi = u[:half], u[half:], f[:half], f[half:]
    return fold(ur * fr + ui * fi), fold(ur * fi - ui * fr)


def removed_part(u, re, im):
    half = u.shape[0] // 2
    ur, ui = u[:half], u[half:]
    return jnp.concatenate([re * ur - im * ui, re * ui + im * ur], axis=0)


def mm(a, b):
    return jnp.dot(a, b, preferred_element_type=F32)


def kernel(
    G, X, B, depth,
    res_in, rit_in, den_in, pml_in, msk_in, kb_in, kr_in, kp_in, kf_in, sre, sim,
    cor, fil,
    res, rit, den, pml, msk, kb, kr, kp, kf, R, U,
    kface, kself, hsend, hrecv, V, H, I1, st, st2, p1, p2,
    sens, zrecv, zpad, lat, lrecv, wlat,
    ins, s1s, s1r, s2s, s2r, hss, hrs, zss, zrs, lss, lrs,
):
    g = lax.axis_index("gz")
    t = lax.axis_index("xy")
    col = lax.rem(t, TX)
    row = t // TX
    TY = X // TX
    count = float(B * depth * LANES * G * X)

    loads = [
        pltpu.make_async_copy(src, dst, ins.at[n])
        for n, (src, dst) in enumerate((
            (rit_in, rit), (res_in, res), (kf_in, kf), (kb_in, kb), (kr_in, kr), (kp_in, kp),
            (den_in, den), (pml_in, pml), (msk_in, msk),
        ))
    ]
    for copy in loads:
        copy.start()

    def gz_peer(o):
        return {"gz": lax.rem(g + o + G, G)}

    def xy_peer(o):
        return {"xy": lax.rem(t + o + X, X)}

    barrier = pltpu.get_barrier_semaphore()
    for o in range(1, G):
        pl.semaphore_signal(barrier, inc=1, device_id=gz_peer(o), device_id_type=MESH)
    for o in range(1, X):
        pl.semaphore_signal(barrier, inc=1, device_id=xy_peer(o), device_id_type=MESH)

    def rlayer(ref, z):
        return ref[pl.ds(z, B, stride=depth), :]

    def remote(src, dst, ss, rs, dev):
        return pltpu.make_async_remote_copy(
            src_ref=src, dst_ref=dst, send_sem=ss, recv_sem=rs,
            device_id=dev, device_id_type=MESH,
        )

    def stage1(r):
        return [
            remote(st.at[r], p1.at[r, o - 1], s1s.at[r, o - 1], s1r.at[r, o - 1], gz_peer(o))
            for o in range(1, G)
        ]

    def stage2(r):
        return [
            remote(st2.at[r], p2.at[r, o - 1], s2s.at[r, o - 1], s2r.at[r, o - 1], xy_peer(o))
            for o in range(1, X)
        ]

    def sum_start(r, a, b, c):
        rows = [jnp.sum(v, axis=0, keepdims=True) for v in (a, b, c)]
        st[r] = jnp.concatenate(rows + [jnp.zeros((5, LANES), F32)], axis=0)
        for copy in stage1(r):
            copy.start()

    def sum_middle(r):
        for copy in stage1(r):
            copy.wait()
        total = st[r]
        for o in range(G - 1):
            total = total + p1[r, o]
        st2[r] = total
        for copy in stage2(r):
            copy.start()

    def sum_end(r):
        for copy in stage2(r):
            copy.wait()
        total = st2[r]
        for o in range(X - 1):
            total = total + p2[r, o]
        total = jnp.sum(total, axis=1, keepdims=True)
        return total[0:1], total[1:2], total[2:3]

    faces = [
        (gz_peer(-1), g > 0, g < G - 1),
        (gz_peer(1), g < G - 1, g > 0),
        (xy_peer(-TX), row > 0, row < TY - 1),
        (xy_peer(TX), row < TY - 1, row > 0),
        (xy_peer(-1), col > 0, col < TX - 1),
        (xy_peer(1), col < TX - 1, col > 0),
    ]

    def halo(s, k):
        src = (R, U, I1)[s].at[(0, depth - 1)[k]] if k < 2 else hsend.at[s, k - 2]
        return remote(src, hrecv.at[s, k], hss.at[s, k], hrs.at[s, k], faces[k][0])

    def halo_start(s, ks):
        for k in ks:
            @pl.when(faces[k][1])
            def _(k=k):
                halo(s, k).start()

    def halo_wait(s):
        for k in range(6):
            @pl.when(faces[k][1])
            def _(k=k):
                halo(s, k).wait_send()

            @pl.when(faces[k][2])
            def _(k=k):
                halo(s, k).wait_recv()

    lane = lax.broadcasted_iota(jnp.int32, (1, LANES), 1)
    lane_x = lane % EX
    lane_y = lane // EX

    def pack(s, load):
        def step(z, carry):
            a, b, c, d = carry
            f = load(z)
            in_y = lane_y == z
            in_x = lane_x == z
            a = jnp.where(in_y, pltpu.roll(f, EX * z, 1), a)
            b = jnp.where(in_y, pltpu.roll(f, lax.rem(EX * z + EX, LANES), 1), b)
            c = jnp.where(in_x, pltpu.roll(f, z, 1), c)
            d = jnp.where(in_x, pltpu.roll(f, lax.rem(z + LANES - EX + 1, LANES), 1), d)
            return a, b, c, d

        def loop(z, carry):
            hs = step(z, tuple(hsend[s, k] for k in range(4)))
            for k in range(4):
                hsend[s, k] = hs[k]
            return carry

        for k in range(4):
            hsend[s, k] = jnp.zeros((B, LANES), F32)
        lax.fori_loop(0, depth, loop, 0)

    half_rows = B * depth // 2
    chunk = half_rows // 8

    def first_sums(i, carry):
        a, b, c = carry
        lo = pl.ds(pl.multiple_of(i * chunk, 8), chunk)
        hi = pl.ds(pl.multiple_of(half_rows + i * chunk, 8), chunk)
        ur, ui, fr, fi = rit[lo, :], rit[hi, :], res[lo, :], res[hi, :]
        return (
            a + fold(ur * ur + ui * ui),
            b + fold(ur * fr + ui * fi),
            c + fold(ur * fi - ui * fr),
        )

    zero = jnp.zeros((8, LANES), F32)
    loads[0].wait()
    loads[1].wait()
    sums = lax.fori_loop(0, 8, first_sums, (zero, zero, zero))
    pl.semaphore_wait(barrier, G - 1 + X - 1)
    sum_start(0, *sums)

    for s, ref, layers in ((0, res, R), (1, rit, U)):
        for k, z in ((0, 0), (1, depth - 1)):
            layers[z] = rlayer(ref, z)
        halo_start(s, (0, 1))

        def turned(z, ref=ref, layers=layers):
            f = rlayer(ref, z)

            @pl.when((z > 0) & (z < depth - 1))
            def _():
                layers[z] = f

            return f

        pack(s, turned)
        if s == 0:
            sum_middle(0)
        halo_start(s, (2, 3, 4, 5))

    for k in range(6):
        @pl.when(jnp.logical_not(faces[k][2]))
        def _(k=k):
            for s in range(3):
                hrecv[s, k] = jnp.zeros((B, LANES), F32)

    for copy in loads[2:]:
        copy.wait()
    fh, fl = split(jnp.concatenate([kf[n] for n in range(6)], axis=1))
    kface[0:B, :] = fh
    kface[B:2 * B, :] = fl
    ri = lax.broadcasted_iota(jnp.int32, (B, B), 0)
    ci = lax.broadcasted_iota(jnp.int32, (B, B), 1)
    half = B // 2
    shift = (
        jnp.where(ri == ci, sre[0, 0], 0.0)
        + jnp.where(ri == ci + half, sim[0, 0], 0.0)
        - jnp.where(ri + half == ci, sim[0, 0], 0.0)
    )
    for n, block in enumerate((kb[...] - shift, kr[...], kp[...])):
        bh, bl = (v.astype(F32) for v in split(block))
        kself[n * B:(n + 1) * B, :] = jnp.concatenate([bh, bh, bl], axis=1).astype(BF16)

    ci = lax.broadcasted_iota(jnp.int32, (LANES, LANES), 0)
    co = lax.broadcasted_iota(jnp.int32, (LANES, LANES), 1)
    for k in range(9):
        dy, dx = k // 3 - 1, k % 3 - 1
        oy = jnp.abs(ci // EX + EY * dy - co // EX)
        ox = jnp.abs(ci % EX + EX * dx - co % EX)
        w = jnp.maximum(REACH + 1 - oy, 0) * jnp.maximum(REACH + 1 - ox, 0)
        wlat[k * LANES:(k + 1) * LANES, :] = w.astype(F32).astype(BF16)

    def build(s, load, scale, re, im):
        def layer(z, carry):
            V[z + 1] = scale * (load(z) - removed_part(U[z], re, im))
            return carry

        lax.fori_loop(0, depth, layer, 0)
        halo_wait(s)
        for k in range(6):
            h = scale * (hrecv[s, k] - removed_part(hrecv[1, k], re, im))
            if k == 0:
                V[depth + 1] = h
            elif k == 1:
                V[0] = h
            else:
                H[k - 2] = h

    def image(j):
        lists = [[], [], [], [], [], [], []]
        for q in range(2):
            z = 2 * j + q
            c = V[z + 1]
            yp = jnp.where(lane_y == EY - 1, pltpu.roll(H[0], LANES - EX - EX * z, 1), pltpu.roll(c, LANES - EX, 1))
            ym = jnp.where(lane_y == 0, pltpu.roll(H[1], lax.rem(LANES - EX * z, LANES), 1), pltpu.roll(c, EX, 1))
            xp = jnp.where(lane_x == EX - 1, pltpu.roll(H[2], EX - 1 - z, 1), pltpu.roll(c, LANES - 1, 1))
            xm = jnp.where(lane_x == 0, pltpu.roll(H[3], lax.rem(LANES - z, LANES), 1), pltpu.roll(c, 1, 1))
            for entry, v in zip(lists, (c, V[z + 2], V[z], yp, ym, xp, xm)):
                entry.append(v)
        parts = [split(jnp.concatenate(e, axis=1)) for e in lists]
        fh = jnp.concatenate([p[0] for p in parts[1:]], axis=0)
        fl = jnp.concatenate([p[1] for p in parts[1:]], axis=0)
        both = mm(kface[...], fh)
        total = both[:B] + both[B:] + mm(kface[0:B, :], fl)
        ch, cl = parts[0]
        own = mm(kself[...], jnp.concatenate([ch, cl, ch], axis=0))
        d = jnp.concatenate([den[pl.ds(2 * j, 1), :], den[pl.ds(2 * j + 1, 1), :]], axis=1)
        p = jnp.concatenate([pml[pl.ds(2 * j, 1), :], pml[pl.ds(2 * j + 1, 1), :]], axis=1).astype(F32)
        rho = own[B:2 * B]
        return total + own[:B] + d * rho + p * own[2 * B:], rho

    norm, re, im = sum_end(0)
    inv = 1.0 / norm
    halo_wait(1)
    build(0, lambda z: R[z], 1.0, re * inv, im * inv)

    def apply_one(j, carry):
        a, b, c = carry
        out, unused = image(j)
        for q in range(2):
            z = 2 * j + q
            o = out[:, q * LANES:(q + 1) * LANES]
            I1[z] = o
            re_q, im_q = pair_terms(U[z], o)
            a, b, c = a + re_q, b + im_q, c + fold(o * o)
        return a, b, c

    sums = lax.fori_loop(0, depth // 2, apply_one, (zero, zero, zero))
    sum_start(1, *sums)
    halo_start(2, (0, 1))
    pack(2, lambda z: I1[z])
    sum_middle(1)
    halo_start(2, (2, 3, 4, 5))
    re, im, square = sum_end(1)
    factor = jnp.sqrt(count / (square - (re * re + im * im) * inv))
    build(2, lambda z: I1[z], factor, re * inv, im * inv)

    def apply_two(j, carry):
        a, b = carry
        out, rho = image(j)
        for q in range(2):
            z = 2 * j + q
            o = out[:, q * LANES:(q + 1) * LANES]
            r = rho[:, q * LANES:(q + 1) * LANES]
            I1[z] = o
            u = U[z]
            re_q, im_q = pair_terms(u, o)
            a, b = a + re_q, b + im_q
            w = msk[pl.ds(z, 1), :].astype(F32) * (1.0 / 36.0)
            br, bi = pair_terms(u, r)
            for n, v in enumerate((fold(o * r), br, bi)):
                sens[n, pl.ds(z, 1), :] = jnp.sum(v, axis=0, keepdims=True) * w
        return a, b

    a, b = lax.fori_loop(0, depth // 2, apply_two, (zero, zero))
    sum_start(2, a, b, zero)

    def zcopy(k):
        return remote(sens, zrecv.at[k], zss.at[k], zrs.at[k], faces[k][0])

    for k in range(2):
        @pl.when(faces[k][1])
        def _(k=k):
            zcopy(k).start()

        @pl.when(jnp.logical_not(faces[k][2]))
        def _(k=k):
            zrecv[k] = jnp.zeros((3, depth, LANES), F32)

    sum_middle(2)
    for k in range(2):
        @pl.when(faces[k][1])
        def _(k=k):
            zcopy(k).wait_send()

        @pl.when(faces[k][2])
        def _(k=k):
            zcopy(k).wait_recv()
    for n in range(3):
        zpad[n, 0:depth, :] = zrecv[1, n]
        zpad[n, depth:2 * depth, :] = sens[n]
        zpad[n, 2 * depth:3 * depth, :] = zrecv[0, n]
        total = jnp.zeros((depth, LANES), F32)
        for d in range(-REACH, REACH + 1):
            total = total + ((REACH + 1.0 - abs(d)) / 12.0) * zpad[n, depth + d:2 * depth + d, :]
        lat[n * depth:(n + 1) * depth, :] = total

    lateral = []
    for k in range(9):
        if k == 4:
            continue
        dy, dx = k // 3 - 1, k % 3 - 1
        gets = (row + dy >= 0) & (row + dy < TY) & (col + dx >= 0) & (col + dx < TX)
        gives = (row - dy >= 0) & (row - dy < TY) & (col - dx >= 0) & (col - dx < TX)
        copy = remote(lat, lrecv.at[k], lss.at[k], lrs.at[k], xy_peer(-dy * TX - dx))
        lateral.append((k, gets, gives, copy))
    for k, gets, gives, copy in lateral:
        @pl.when(gives)
        def _(copy=copy):
            copy.start()

        @pl.when(jnp.logical_not(gets))
        def _(k=k):
            lrecv[k] = jnp.zeros((3 * depth, LANES), F32)
    lrecv[4] = lat[...]

    re, im, unused = sum_end(2)
    re, im = re * inv, im * inv

    def finish(z, carry):
        cor[pl.ds(z, B, stride=depth), :] = I1[z] - removed_part(U[z], re, im)
        return carry

    lax.fori_loop(0, depth, finish, 0)
    for k, gets, gives, copy in lateral:
        @pl.when(gives)
        def _(copy=copy):
            copy.wait_send()

        @pl.when(gets)
        def _(copy=copy):
            copy.wait_recv()
    tiles = jnp.concatenate([lrecv[k] for k in range(9)], axis=1)
    th, tl = split(tiles)
    smooth = (mm(th, wlat[...]) + mm(tl, wlat[...])) * (1.0 / 144.0)
    fil[...] = smooth[:depth] - re * smooth[depth:2 * depth] - im * smooth[2 * depth:]


def local(G, X, residual_in, ritz_vector, density, pml_flags, design_mask, k_base, k_rho, k_pml, k_face, shift_re, shift_im):
    B, depth = residual_in.shape[:2]
    vmem = pl.BlockSpec(memory_space=pltpu.VMEM)
    smem = pl.BlockSpec(memory_space=pltpu.SMEM)
    dma = pltpu.SemaphoreType.DMA
    field = (B, LANES)
    correction, filtered = pl.pallas_call(
        functools.partial(kernel, G, X, B, depth),
        out_shape=(
            pltpu.VMEM((B * depth, LANES), F32),
            pltpu.VMEM((depth, LANES), F32),
        ),
        in_specs=[pl.BlockSpec(memory_space=pltpu.HBM)] * 9 + [smem] * 2,
        out_specs=(vmem, vmem),
        scratch_shapes=[
            pltpu.VMEM((B * depth, LANES), F32),
            pltpu.VMEM((B * depth, LANES), F32),
            pltpu.VMEM((depth, LANES), F32),
            pltpu.VMEM((depth, LANES), jnp.int32),
            pltpu.VMEM((depth, LANES), jnp.int32),
            pltpu.VMEM((B, B), F32),
            pltpu.VMEM((B, B), F32),
            pltpu.VMEM((B, B), F32),
            pltpu.VMEM((6, B, B), F32),
            pltpu.VMEM((depth,) + field, F32),
            pltpu.VMEM((depth,) + field, F32),
            pltpu.VMEM((2 * B, 6 * B), BF16),
            pltpu.VMEM((3 * B, 3 * B), BF16),
            pltpu.VMEM((3, 4) + field, F32),
            pltpu.VMEM((3, 6) + field, F32),
            pltpu.VMEM((depth + 2,) + field, F32),
            pltpu.VMEM((4,) + field, F32),
            pltpu.VMEM((depth,) + field, F32),
            pltpu.VMEM((3, 8, LANES), F32),
            pltpu.VMEM((3, 8, LANES), F32),
            pltpu.VMEM((3, G - 1, 8, LANES), F32),
            pltpu.VMEM((3, X - 1, 8, LANES), F32),
            pltpu.VMEM((3, depth, LANES), F32),
            pltpu.VMEM((2, 3, depth, LANES), F32),
            pltpu.VMEM((3, 3 * depth, LANES), F32),
            pltpu.VMEM((3 * depth, LANES), F32),
            pltpu.VMEM((9, 3 * depth, LANES), F32),
            pltpu.VMEM((9 * LANES, LANES), BF16),
            dma((9,)),
            dma((3, G - 1)),
            dma((3, G - 1)),
            dma((3, X - 1)),
            dma((3, X - 1)),
            dma((3, 6)),
            dma((3, 6)),
            dma((2,)),
            dma((2,)),
            dma((9,)),
            dma((9,)),
        ],
        compiler_params=pltpu.CompilerParams(
            collective_id=0, has_side_effects=True, vmem_limit_bytes=40 * 1024 * 1024
        ),
    )(
        *(
            pltpu.with_memory_space_constraint(x, pltpu.HBM)
            for x in (
                residual_in.reshape(B * depth, LANES),
                ritz_vector.reshape(B * depth, LANES),
                density.reshape(depth, LANES),
                pml_flags.reshape(depth, LANES),
                design_mask.reshape(depth, LANES),
                k_base, k_rho, k_pml, k_face,
            )
        ),
        shift_re.reshape(1, 1), shift_im.reshape(1, 1),
    )
    return correction.reshape(residual_in.shape), filtered.reshape(density.shape)


def solution(mesh):
    wide = P(None, "gz", "xy", None)
    flat = P("gz", "xy", None)
    return jax.shard_map(
        functools.partial(local, mesh.shape["gz"], mesh.shape["xy"]),
        mesh=mesh,
        in_specs=(wide, wide, flat, flat, flat, P(), P(), P(), P(), P(), P()),
        out_specs=(wide, flat),
        check_vma=False,
    )
```

```python
import functools

import jax
import jax.numpy as jnp
from jax import lax
from jax.experimental import pallas as pl
from jax.experimental.pallas import tpu as pltpu
from jax.sharding import PartitionSpec as P

TX = 4
EY = 8
EX = 16
LANES = EY * EX
REACH = 5
MESH = pl.DeviceIdType.MESH
F32 = jnp.float32
BF16 = jnp.bfloat16


def split(x):
    hi = x.astype(BF16)
    return hi, (x - hi.astype(F32)).astype(BF16)


def fold(x):
    return jnp.sum(x.reshape(x.shape[0] // 8, 8, LANES), axis=0)


def pair_terms(u, f):
    half = u.shape[0] // 2
    ur, ui, fr, fi = u[:half], u[half:], f[:half], f[half:]
    return fold(ur * fr + ui * fi), fold(ur * fi - ui * fr)


def removed_part(u, re, im):
    half = u.shape[0] // 2
    ur, ui = u[:half], u[half:]
    return jnp.concatenate([re * ur - im * ui, re * ui + im * ur], axis=0)


def mm(a, b):
    return jnp.dot(a, b, preferred_element_type=F32)


def kernel(
    G, X, B, depth,
    res_in, rit_in, den_in, pml_in, msk_in, kb_in, kr_in, kp_in, kf_in, sre, sim,
    cor, fil,
    res, rit, den, pml, msk, kb, kr, kp, kf, R, U,
    kface, kself, hsend, hrecv, V, H, I1, st, st2, p1, p2,
    sens, zrecv, zpad, lat, lrecv, wlat,
    ins, s1s, s1r, s2s, s2r, hss, hrs, zss, zrs, lss, lrs,
):
    g = lax.axis_index("gz")
    t = lax.axis_index("xy")
    col = lax.rem(t, TX)
    row = t // TX
    TY = X // TX
    count = float(B * depth * LANES * G * X)

    loads = [
        pltpu.make_async_copy(src, dst, ins.at[n])
        for n, (src, dst) in enumerate((
            (rit_in, rit), (res_in, res), (kf_in, kf), (kb_in, kb), (kr_in, kr), (kp_in, kp),
            (den_in, den), (pml_in, pml), (msk_in, msk),
        ))
    ]
    for copy in loads:
        copy.start()

    def gz_peer(o):
        return {"gz": lax.rem(g + o + G, G)}

    def xy_peer(o):
        return {"xy": lax.rem(t + o + X, X)}

    barrier = pltpu.get_barrier_semaphore()
    for o in range(1, G):
        pl.semaphore_signal(barrier, inc=1, device_id=gz_peer(o), device_id_type=MESH)
    for o in range(1, X):
        pl.semaphore_signal(barrier, inc=1, device_id=xy_peer(o), device_id_type=MESH)

    def rlayer(ref, z):
        return ref[pl.ds(z, B, stride=depth), :]

    def remote(src, dst, ss, rs, dev):
        return pltpu.make_async_remote_copy(
            src_ref=src, dst_ref=dst, send_sem=ss, recv_sem=rs,
            device_id=dev, device_id_type=MESH,
        )

    def stage1(r):
        return [
            remote(st.at[r], p1.at[r, o - 1], s1s.at[r, o - 1], s1r.at[r, o - 1], gz_peer(o))
            for o in range(1, G)
        ]

    def stage2(r):
        return [
            remote(st2.at[r], p2.at[r, o - 1], s2s.at[r, o - 1], s2r.at[r, o - 1], xy_peer(o))
            for o in range(1, X)
        ]

    def sum_start(r, a, b, c):
        rows = [jnp.sum(v, axis=0, keepdims=True) for v in (a, b, c)]
        st[r] = jnp.concatenate(rows + [jnp.zeros((5, LANES), F32)], axis=0)
        for copy in stage1(r):
            copy.start()

    def sum_middle(r):
        for copy in stage1(r):
            copy.wait()
        total = st[r]
        for o in range(G - 1):
            total = total + p1[r, o]
        st2[r] = total
        for copy in stage2(r):
            copy.start()

    def sum_end(r):
        for copy in stage2(r):
            copy.wait()
        total = st2[r]
        for o in range(X - 1):
            total = total + p2[r, o]
        total = jnp.sum(total, axis=1, keepdims=True)
        return total[0:1], total[1:2], total[2:3]

    faces = [
        (gz_peer(-1), g > 0, g < G - 1),
        (gz_peer(1), g < G - 1, g > 0),
        (xy_peer(-TX), row > 0, row < TY - 1),
        (xy_peer(TX), row < TY - 1, row > 0),
        (xy_peer(-1), col > 0, col < TX - 1),
        (xy_peer(1), col < TX - 1, col > 0),
    ]

    def halo(s, k):
        src = (R, U, I1)[s].at[(0, depth - 1)[k]] if k < 2 else hsend.at[s, k - 2]
        return remote(src, hrecv.at[s, k], hss.at[s, k], hrs.at[s, k], faces[k][0])

    def halo_start(s, ks):
        for k in ks:
            @pl.when(faces[k][1])
            def _(k=k):
                halo(s, k).start()

    def halo_wait(s):
        for k in range(6):
            @pl.when(faces[k][1])
            def _(k=k):
                halo(s, k).wait_send()

            @pl.when(faces[k][2])
            def _(k=k):
                halo(s, k).wait_recv()

    lane = lax.broadcasted_iota(jnp.int32, (1, LANES), 1)
    lane_x = lane % EX
    lane_y = lane // EX

    def pack(s, z, f):
        in_y = lane_y == z
        in_x = lane_x == z
        turned = (
            (in_y, pltpu.roll(f, EX * z, 1)),
            (in_y, pltpu.roll(f, lax.rem(EX * z + EX, LANES), 1)),
            (in_x, pltpu.roll(f, z, 1)),
            (in_x, pltpu.roll(f, lax.rem(z + LANES - EX + 1, LANES), 1)),
        )
        for k, (where, v) in enumerate(turned):
            hsend[s, k] = jnp.where(where, v, hsend[s, k])

    blank = jnp.zeros((B, LANES), F32)
    for s in range(3):
        for k in range(4):
            hsend[s, k] = blank

    def first_pass(z, carry):
        a, b, c = carry
        u, f = rlayer(rit, z), rlayer(res, z)
        U[z] = u
        R[z] = f
        pack(0, z, f)
        pack(1, z, u)
        re_z, im_z = pair_terms(u, f)
        return a + fold(u * u), b + re_z, c + im_z

    zero = jnp.zeros((8, LANES), F32)
    loads[0].wait()
    loads[1].wait()
    sums = lax.fori_loop(0, depth, first_pass, (zero, zero, zero))
    pl.semaphore_wait(barrier, G - 1 + X - 1)
    sum_start(0, *sums)
    for ks in ((2, 3), (0, 1), (4, 5)):
        for s in range(2):
            halo_start(s, ks)
    sum_middle(0)

    for k in range(6):
        @pl.when(jnp.logical_not(faces[k][2]))
        def _(k=k):
            for s in range(3):
                hrecv[s, k] = jnp.zeros((B, LANES), F32)

    for copy in loads[2:]:
        copy.wait()
    fh, fl = split(jnp.concatenate([kf[n] for n in range(6)], axis=1))
    kface[0:B, :] = fh
    kface[B:2 * B, :] = fl
    ri = lax.broadcasted_iota(jnp.int32, (B, B), 0)
    ci = lax.broadcasted_iota(jnp.int32, (B, B), 1)
    half = B // 2
    shift = (
        jnp.where(ri == ci, sre[0, 0], 0.0)
        + jnp.where(ri == ci + half, sim[0, 0], 0.0)
        - jnp.where(ri + half == ci, sim[0, 0], 0.0)
    )
    for n, block in enumerate((kb[...] - shift, kr[...], kp[...])):
        bh, bl = (v.astype(F32) for v in split(block))
        kself[n * B:(n + 1) * B, :] = jnp.concatenate([bh, bh, bl], axis=1).astype(BF16)

    ci = lax.broadcasted_iota(jnp.int32, (LANES, LANES), 0)
    co = lax.broadcasted_iota(jnp.int32, (LANES, LANES), 1)
    for k in range(9):
        dy, dx = k // 3 - 1, k % 3 - 1
        oy = jnp.abs(ci // EX + EY * dy - co // EX)
        ox = jnp.abs(ci % EX + EX * dx - co % EX)
        w = jnp.maximum(REACH + 1 - oy, 0) * jnp.maximum(REACH + 1 - ox, 0)
        wlat[k * LANES:(k + 1) * LANES, :] = w.astype(F32).astype(BF16)

    def build(s, load, scale, re, im):
        def layer(z, carry):
            V[z + 1] = scale * (load(z) - removed_part(U[z], re, im))
            return carry

        lax.fori_loop(0, depth, layer, 0)
        halo_wait(s)
        for k in range(6):
            h = scale * (hrecv[s, k] - removed_part(hrecv[1, k], re, im))
            if k == 0:
                V[depth + 1] = h
            elif k == 1:
                V[0] = h
            else:
                H[k - 2] = h

    def image(j):
        lists = [[], [], [], [], [], [], []]
        for q in range(2):
            z = 2 * j + q
            c = V[z + 1]
            yp = jnp.where(lane_y == EY - 1, pltpu.roll(H[0], LANES - EX - EX * z, 1), pltpu.roll(c, LANES - EX, 1))
            ym = jnp.where(lane_y == 0, pltpu.roll(H[1], lax.rem(LANES - EX * z, LANES), 1), pltpu.roll(c, EX, 1))
            xp = jnp.where(lane_x == EX - 1, pltpu.roll(H[2], EX - 1 - z, 1), pltpu.roll(c, LANES - 1, 1))
            xm = jnp.where(lane_x == 0, pltpu.roll(H[3], lax.rem(LANES - z, LANES), 1), pltpu.roll(c, 1, 1))
            for entry, v in zip(lists, (c, V[z + 2], V[z], yp, ym, xp, xm)):
                entry.append(v)
        parts = [split(jnp.concatenate(e, axis=1)) for e in lists]
        fh = jnp.concatenate([p[0] for p in parts[1:]], axis=0)
        fl = jnp.concatenate([p[1] for p in parts[1:]], axis=0)
        both = mm(kface[...], fh)
        total = both[:B] + both[B:] + mm(kface[0:B, :], fl)
        ch, cl = parts[0]
        own = mm(kself[...], jnp.concatenate([ch, cl, ch], axis=0))
        d = jnp.concatenate([den[pl.ds(2 * j, 1), :], den[pl.ds(2 * j + 1, 1), :]], axis=1)
        p = jnp.concatenate([pml[pl.ds(2 * j, 1), :], pml[pl.ds(2 * j + 1, 1), :]], axis=1).astype(F32)
        rho = own[B:2 * B]
        return total + own[:B] + d * rho + p * own[2 * B:], rho

    norm, re, im = sum_end(0)
    inv = 1.0 / norm
    halo_wait(1)
    build(0, lambda z: R[z], 1.0, re * inv, im * inv)

    def apply_one(j, carry):
        a, b, c = carry
        out, unused = image(j)
        for q in range(2):
            z = 2 * j + q
            o = out[:, q * LANES:(q + 1) * LANES]
            I1[z] = o
            pack(2, z, o)
            re_q, im_q = pair_terms(U[z], o)
            a, b, c = a + re_q, b + im_q, c + fold(o * o)
        return a, b, c

    sums = lax.fori_loop(0, depth // 2, apply_one, (zero, zero, zero))
    sum_start(1, *sums)
    halo_start(2, (2, 3, 0, 1, 4, 5))
    sum_middle(1)
    re, im, square = sum_end(1)
    factor = jnp.sqrt(count / (square - (re * re + im * im) * inv))
    build(2, lambda z: I1[z], factor, re * inv, im * inv)

    def apply_two(j, carry):
        a, b = carry
        out, rho = image(j)
        for q in range(2):
            z = 2 * j + q
            o = out[:, q * LANES:(q + 1) * LANES]
            r = rho[:, q * LANES:(q + 1) * LANES]
            I1[z] = o
            u = U[z]
            re_q, im_q = pair_terms(u, o)
            a, b = a + re_q, b + im_q
            w = msk[pl.ds(z, 1), :].astype(F32) * (1.0 / 36.0)
            br, bi = pair_terms(u, r)
            for n, v in enumerate((fold(o * r), br, bi)):
                sens[n, pl.ds(z, 1), :] = jnp.sum(v, axis=0, keepdims=True) * w
        return a, b

    a, b = lax.fori_loop(0, depth // 2, apply_two, (zero, zero))
    sum_start(2, a, b, zero)

    def zcopy(k):
        return remote(sens, zrecv.at[k], zss.at[k], zrs.at[k], faces[k][0])

    for k in range(2):
        @pl.when(faces[k][1])
        def _(k=k):
            zcopy(k).start()

        @pl.when(jnp.logical_not(faces[k][2]))
        def _(k=k):
            zrecv[k] = jnp.zeros((3, depth, LANES), F32)

    sum_middle(2)
    for k in range(2):
        @pl.when(faces[k][1])
        def _(k=k):
            zcopy(k).wait_send()

        @pl.when(faces[k][2])
        def _(k=k):
            zcopy(k).wait_recv()
    for n in range(3):
        zpad[n, 0:depth, :] = zrecv[1, n]
        zpad[n, depth:2 * depth, :] = sens[n]
        zpad[n, 2 * depth:3 * depth, :] = zrecv[0, n]
        total = jnp.zeros((depth, LANES), F32)
        for d in range(-REACH, REACH + 1):
            total = total + ((REACH + 1.0 - abs(d)) / 12.0) * zpad[n, depth + d:2 * depth + d, :]
        lat[n * depth:(n + 1) * depth, :] = total

    lateral = []
    for k in range(9):
        if k == 4:
            continue
        dy, dx = k // 3 - 1, k % 3 - 1
        gets = (row + dy >= 0) & (row + dy < TY) & (col + dx >= 0) & (col + dx < TX)
        gives = (row - dy >= 0) & (row - dy < TY) & (col - dx >= 0) & (col - dx < TX)
        copy = remote(lat, lrecv.at[k], lss.at[k], lrs.at[k], xy_peer(-dy * TX - dx))
        lateral.append((k, gets, gives, copy))
    for k, gets, gives, copy in lateral:
        @pl.when(gives)
        def _(copy=copy):
            copy.start()

        @pl.when(jnp.logical_not(gets))
        def _(k=k):
            lrecv[k] = jnp.zeros((3 * depth, LANES), F32)
    lrecv[4] = lat[...]

    re, im, unused = sum_end(2)
    re, im = re * inv, im * inv

    def finish(z, carry):
        cor[pl.ds(z, B, stride=depth), :] = I1[z] - removed_part(U[z], re, im)
        return carry

    lax.fori_loop(0, depth, finish, 0)
    for k, gets, gives, copy in lateral:
        @pl.when(gives)
        def _(copy=copy):
            copy.wait_send()

        @pl.when(gets)
        def _(copy=copy):
            copy.wait_recv()
    tiles = jnp.concatenate([lrecv[k] for k in range(9)], axis=1)
    th, tl = split(tiles)
    smooth = (mm(th, wlat[...]) + mm(tl, wlat[...])) * (1.0 / 144.0)
    fil[...] = smooth[:depth] - re * smooth[depth:2 * depth] - im * smooth[2 * depth:]


def local(G, X, residual_in, ritz_vector, density, pml_flags, design_mask, k_base, k_rho, k_pml, k_face, shift_re, shift_im):
    B, depth = residual_in.shape[:2]
    vmem = pl.BlockSpec(memory_space=pltpu.VMEM)
    smem = pl.BlockSpec(memory_space=pltpu.SMEM)
    dma = pltpu.SemaphoreType.DMA
    field = (B, LANES)
    correction, filtered = pl.pallas_call(
        functools.partial(kernel, G, X, B, depth),
        out_shape=(
            pltpu.VMEM((B * depth, LANES), F32),
            pltpu.VMEM((depth, LANES), F32),
        ),
        in_specs=[pl.BlockSpec(memory_space=pltpu.HBM)] * 9 + [smem] * 2,
        out_specs=(vmem, vmem),
        scratch_shapes=[
            pltpu.VMEM((B * depth, LANES), F32),
            pltpu.VMEM((B * depth, LANES), F32),
            pltpu.VMEM((depth, LANES), F32),
            pltpu.VMEM((depth, LANES), jnp.int32),
            pltpu.VMEM((depth, LANES), jnp.int32),
            pltpu.VMEM((B, B), F32),
            pltpu.VMEM((B, B), F32),
            pltpu.VMEM((B, B), F32),
            pltpu.VMEM((6, B, B), F32),
            pltpu.VMEM((depth,) + field, F32),
            pltpu.VMEM((depth,) + field, F32),
            pltpu.VMEM((2 * B, 6 * B), BF16),
            pltpu.VMEM((3 * B, 3 * B), BF16),
            pltpu.VMEM((3, 4) + field, F32),
            pltpu.VMEM((3, 6) + field, F32),
            pltpu.VMEM((depth + 2,) + field, F32),
            pltpu.VMEM((4,) + field, F32),
            pltpu.VMEM((depth,) + field, F32),
            pltpu.VMEM((3, 8, LANES), F32),
            pltpu.VMEM((3, 8, LANES), F32),
            pltpu.VMEM((3, G - 1, 8, LANES), F32),
            pltpu.VMEM((3, X - 1, 8, LANES), F32),
            pltpu.VMEM((3, depth, LANES), F32),
            pltpu.VMEM((2, 3, depth, LANES), F32),
            pltpu.VMEM((3, 3 * depth, LANES), F32),
            pltpu.VMEM((3 * depth, LANES), F32),
            pltpu.VMEM((9, 3 * depth, LANES), F32),
            pltpu.VMEM((9 * LANES, LANES), BF16),
            dma((9,)),
            dma((3, G - 1)),
            dma((3, G - 1)),
            dma((3, X - 1)),
            dma((3, X - 1)),
            dma((3, 6)),
            dma((3, 6)),
            dma((2,)),
            dma((2,)),
            dma((9,)),
            dma((9,)),
        ],
        compiler_params=pltpu.CompilerParams(
            collective_id=0, has_side_effects=True, vmem_limit_bytes=40 * 1024 * 1024
        ),
    )(
        *(
            pltpu.with_memory_space_constraint(x, pltpu.HBM)
            for x in (
                residual_in.reshape(B * depth, LANES),
                ritz_vector.reshape(B * depth, LANES),
                density.reshape(depth, LANES),
                pml_flags.reshape(depth, LANES),
                design_mask.reshape(depth, LANES),
                k_base, k_rho, k_pml, k_face,
            )
        ),
        shift_re.reshape(1, 1), shift_im.reshape(1, 1),
    )
    return correction.reshape(residual_in.shape), filtered.reshape(density.shape)


def solution(mesh):
    wide = P(None, "gz", "xy", None)
    flat = P("gz", "xy", None)
    return jax.shard_map(
        functools.partial(local, mesh.shape["gz"], mesh.shape["xy"]),
        mesh=mesh,
        in_specs=(wide, wide, flat, flat, flat, P(), P(), P(), P(), P(), P()),
        out_specs=(wide, flat),
        check_vma=False,
    )
```
